128 devices in a mesh: group: 8 (over z, core), patch: 16 (over y, x).
Axes of the slice: x: 4, y: 4, z: 4, core: 2. Of those that a mesh axis runs over, the one named last changes fastest.
Arguments:
- volume: float32 [4096, 8, 1024], P(('group', 'patch')), may hold values from 0.02 to 18, as said below
- block_place: int32 [4096], P(('group', 'patch')), may hold values from 0 to 4095, as said below
- measured: float32 [2, 512, 384], P(None, 'patch'), may hold values from 0.5 to 5.5
- live_rays: int32 [2, 512], replicated, may hold values from 24 to 48
Outputs:
- final_volume: float32 [4096, 8, 1024], P(('group', 'patch'))
- last_residual: float32 [8, 64, 384], P('group', 'patch')
The draws below stay inside these ranges and needn't reach their ends.
Inputs may be any that keep to these rules, and one draw needn't show every extreme that they name: block_place lists the block positions of the 64 x 64 grid in the order of a Hilbert curve over that grid, begun at a drawn point of the curve (continuing from its end to its start) and turned or mirrored by one of the grid's eight symmetries; each position appears once. `volume`: positive.
All inputs are finite; a program needn't handle non-finite values.
Results may differ from the reference program's by a relative error of at most 0.0007.
Values may be sent and summed in bfloat16 or wider, within the bound.
No kernel may reach another device: no remote copies, remote signals or barrier semaphores. Data moves between devices by JAX's collectives and lax.ppermute only.
A program may use at most 128 MiB of HBM per device.

```python
import math
import jax
import jax.numpy as jnp
from jax import lax

NSL = 8
IMG_BLK = 64
BLK_SIDE = 32
RAYS_TILE = 48
NTILE = 64
ANG_SUB = 8
SUBSETS = 2
NBLK = 4096
ROWS = 512
N_GROUP = 8
N_PATCH = 16


def draw_volume(key, part):
    scale_key, texture_key = jax.random.split(jax.random.fold_in(key, 17))
    brightness = jnp.exp(jax.random.uniform(scale_key, (NBLK, 1, 1), jnp.float32, -2.3, 2.3))
    texture = jax.random.uniform(texture_key, (NBLK, NSL, BLK_SIDE * BLK_SIDE), jnp.float32, 0.5, 1.5)
    return brightness * texture


def draw_block_place(key, part):
    symmetry_key, start_key = jax.random.split(jax.random.fold_in(key, 29))
    symmetry = jax.random.randint(symmetry_key, (3,), 0, 2, jnp.int32)
    start = jax.random.randint(start_key, (), 0, NBLK, jnp.int32)
    walk = (jnp.arange(NBLK, dtype=jnp.int32) + start) % NBLK
    column = jnp.zeros((NBLK,), jnp.int32)
    row_pos = jnp.zeros((NBLK,), jnp.int32)
    level = 1
    while level < IMG_BLK:
        right_bit = walk // 2 % 2
        upper_bit = (walk + right_bit) % 2
        upper_bit = jnp.where(right_bit == 1, 1 - walk % 2, walk % 2)
        flipped = (upper_bit == 0) & (right_bit == 1)
        column = jnp.where(flipped, level - 1 - column, column)
        row_pos = jnp.where(flipped, level - 1 - row_pos, row_pos)
        turned = upper_bit == 0
        column, row_pos = (jnp.where(turned, row_pos, column), jnp.where(turned, column, row_pos))
        column = column + level * right_bit
        row_pos = row_pos + level * upper_bit
        walk = walk // 4
        level = level * 2
    column = jnp.where(symmetry[0] == 1, IMG_BLK - 1 - column, column)
    row_pos = jnp.where(symmetry[1] == 1, IMG_BLK - 1 - row_pos, row_pos)
    column, row_pos = (jnp.where(symmetry[2] == 1, row_pos, column), jnp.where(symmetry[2] == 1, column, row_pos))
    return (row_pos * IMG_BLK + column).astype(jnp.int32)


def with_ends(values, key, smallest, largest):
    spot = [jax.random.randint(jax.random.fold_in(key, axis), (), 0, length) for axis, length in enumerate(values.shape)]
    longest = values.shape.index(max(values.shape))
    neighbour = spot[:longest] + [(spot[longest] + 1) % values.shape[longest]] + spot[longest + 1:]
    return values.at[tuple(spot)].set(smallest).at[tuple(neighbour)].set(largest)


def levels(stream_key, dims, shards, low, top_value):
    def one(position, parts):
        steps = jax.random.uniform(jax.random.fold_in(jax.random.fold_in(stream_key, 6), position), (parts,), jnp.float32, low / len(shards), top_value / len(shards))
        return jnp.repeat(jnp.exp(steps), dims[position] // parts).reshape((-1,) + (1,) * (len(dims) - position - 1))

    factor_of = one(*shards[0])
    for cut in shards[1:]:
        factor_of = factor_of * one(*cut)
    return factor_of


def setup_inputs(seed: int = 0) -> dict:
    splits = jax.random.split(jax.random.key(seed), 5)
    volume = draw_volume(jax.random.fold_in(splits[4], 71), 0)
    block_place = draw_block_place(jax.random.fold_in(splits[4], 71), 0)
    measured = jnp.clip(0.5 + 5.0 * jax.random.uniform(splits[2], (SUBSETS, ROWS, RAYS_TILE * NSL), jnp.float32) ** levels(splits[2], (SUBSETS, ROWS, RAYS_TILE * NSL), ((1, 16),), -0.2, 0.2), 0.5, 5.5)
    live_rays = with_ends(jax.random.randint(splits[3], (SUBSETS, ROWS), 24, 49), jax.random.fold_in(splits[3], 1), 24, 48).astype(jnp.int32)
    return {"volume": volume, "block_place": block_place, "measured": measured, "live_rays": live_rays}


spread = 1.5
relax = 0.9


def footprint_tiles(place, angle_value):
    cosine = jnp.cos(angle_value)
    sine_value = jnp.sin(angle_value)
    half_image = IMG_BLK * BLK_SIDE * 0.5
    half_detector = NTILE * RAYS_TILE * 0.5
    block_col = (place % IMG_BLK).astype(jnp.float32) * BLK_SIDE - half_image
    block_row = (place // IMG_BLK).astype(jnp.float32) * BLK_SIDE - half_image
    centre = (block_col + BLK_SIDE * 0.5) * cosine + (block_row + BLK_SIDE * 0.5) * sine_value
    first_tile = jnp.floor((centre + half_detector - RAYS_TILE * 0.5) / RAYS_TILE).astype(jnp.int32)
    voxel = jnp.arange(BLK_SIDE * BLK_SIDE, dtype=jnp.int32)
    offset_col = (voxel % BLK_SIDE).astype(jnp.float32) + 0.5
    offset_row = (voxel // BLK_SIDE).astype(jnp.float32) + 0.5
    along = (block_col[:, None] + offset_col[None, :]) * cosine + (block_row[:, None] + offset_row[None, :]) * sine_value
    ray_ids = first_tile[:, None] * RAYS_TILE + jnp.arange(2 * RAYS_TILE, dtype=jnp.int32)[None, :]
    detector = ray_ids.astype(jnp.float32) + 0.5 - half_detector
    scaled = (along[:, None, :] - detector[:, :, None]) / spread
    bump = jnp.maximum(1.0 - scaled * scaled, 0.0)
    return first_tile, (bump * bump).astype(jnp.bfloat16)


def angle_of(angle, subset):
    return jnp.asarray(math.pi * (angle * SUBSETS + subset) / (ANG_SUB * SUBSETS), jnp.float32)


def tile_rows(angle, first_tile):
    return (angle * NTILE + first_tile[:, None] + jnp.arange(2, dtype=jnp.int32)[None, :]).reshape(-1)


def forward(rounded, place, subset):
    blocks, slices = rounded.shape[0], rounded.shape[1]
    projection = jnp.zeros((ANG_SUB * NTILE, RAYS_TILE * slices), jnp.float32)
    ray_sum = jnp.zeros((ANG_SUB * NTILE, RAYS_TILE), jnp.float32)
    col_sum = jnp.zeros((blocks, BLK_SIDE * BLK_SIDE), jnp.float32)
    for angle in range(ANG_SUB):
        first_tile, footprint = footprint_tiles(place, angle_of(angle, subset))
        row_ids = tile_rows(angle, first_tile)
        contrib = jnp.einsum("brv,bsv->brs", footprint.astype(jnp.float32), rounded.astype(jnp.float32))
        projection = projection.at[row_ids].add(contrib.reshape(2 * blocks, RAYS_TILE * slices))
        ray_part = jnp.sum(footprint.astype(jnp.float32), axis=2)
        ray_sum = ray_sum.at[row_ids].add(ray_part.reshape(2 * blocks, RAYS_TILE))
        col_sum = col_sum + jnp.sum(footprint.astype(jnp.float32), axis=1)
    return projection, ray_sum, col_sum


def backward(residual_b, place, subset):
    blocks = place.shape[0]
    slices = residual_b.shape[1] // RAYS_TILE
    total = jnp.zeros((blocks, slices, BLK_SIDE * BLK_SIDE), jnp.float32)
    for angle in range(ANG_SUB):
        first_tile, footprint = footprint_tiles(place, angle_of(angle, subset))
        picked = residual_b[tile_rows(angle, first_tile)].reshape(blocks, 2 * RAYS_TILE, slices)
        total = total + jnp.einsum("brv,brs->bsv", footprint.astype(jnp.float32), picked.astype(jnp.float32))
    return total


def residual_of(projection, ray_sum, measured_rows, live_count):
    count = projection.shape[0]
    live = (jnp.arange(RAYS_TILE, dtype=jnp.int32)[None, :] < live_count[:, None]).astype(jnp.float32)
    level = projection.reshape(count, RAYS_TILE, -1) / jnp.maximum(ray_sum, 1.0)[:, :, None]
    differ = (measured_rows.reshape(count, RAYS_TILE, -1) - level) * live[:, :, None]
    return differ.reshape(count, -1)


def reference(volume, block_place, measured, live_rays):
    estimate = volume
    slices = volume.shape[1]
    width = RAYS_TILE * slices
    batches = NBLK // 64
    place_groups = block_place.reshape(batches, 64)
    residual = jnp.zeros((ANG_SUB * NTILE, width), jnp.float32)
    for subset in range(SUBSETS):
        rounded = estimate.astype(jnp.bfloat16).reshape(batches, 64, slices, BLK_SIDE * BLK_SIDE)

        def forward_step(totals, member):
            projection, ray_sum, col_sum = forward(member[0], member[1], subset)
            return (totals[0] + projection, totals[1] + ray_sum), col_sum

        start = (jnp.zeros((ANG_SUB * NTILE, width), jnp.float32), jnp.zeros((ANG_SUB * NTILE, RAYS_TILE), jnp.float32))
        totals, col_sums = lax.scan(forward_step, start, (rounded, place_groups))
        col_sum = col_sums.reshape(NBLK, BLK_SIDE * BLK_SIDE)
        residual = residual_of(totals[0], totals[1], measured[subset], live_rays[subset])
        residual_b = residual.astype(jnp.bfloat16)
        backprojected = lax.map(lambda place: backward(residual_b, place, subset), place_groups)
        backprojected = backprojected.reshape(NBLK, slices, BLK_SIDE * BLK_SIDE)
        estimate = jnp.maximum(estimate + relax * backprojected / col_sum[:, None, :], 0.0)
    share_rows = ANG_SUB * NTILE // (N_GROUP * N_PATCH)
    last_residual = residual.reshape(N_PATCH, N_GROUP, share_rows, width).transpose(1, 0, 2, 3)
    return estimate, last_residual.reshape(N_GROUP, N_PATCH * share_rows, width)
```

```python
import functools
import math

import jax
import jax.numpy as jnp
import numpy as np
from jax import lax
from jax.experimental import pallas as pl
from jax.experimental.pallas import tpu as pltpu
from jax.sharding import PartitionSpec as P

IMG_BLK = 64
BLK_SIDE = 32
VOX = BLK_SIDE * BLK_SIDE
RAYS_TILE = 48
NTILE = 64
ANG_SUB = 8
SUBSETS = 2
NSL = 8
SPREAD = 1.5
RELAX = 0.9
RAYS = NTILE * RAYS_TILE
WIN = 48
KALL = ANG_SUB * WIN
HALF_IMG = IMG_BLK * BLK_SIDE * 0.5
CHUNKS = 16
LOCAL = 32
LEAD = 23.75


def angle_consts(subset):
    out = []
    for a in range(ANG_SUB):
        theta = np.float32(math.pi * (a * SUBSETS + subset) / (ANG_SUB * SUBSETS))
        out.append((float(np.cos(theta)), float(np.sin(theta))))
    return out


def touched(cos, sin, ray0, chunk):
    v = np.arange(chunk * 128, chunk * 128 + 128)
    along = (v % BLK_SIDE - 15.5) * cos + (v // BLK_SIDE - 15.5) * sin
    low = along.min() + LEAD - 0.5 - SPREAD - 0.01
    high = along.max() + LEAD + 0.5 + SPREAD + 0.01
    return ray0 <= high and ray0 + 7 >= low


def place_of(place_ref, b, cos, sin):
    q = place_ref[b]
    x = ((q & (IMG_BLK - 1)) * BLK_SIDE).astype(jnp.float32) + (BLK_SIDE * 0.5 - HALF_IMG)
    y = ((q >> 6) * BLK_SIDE).astype(jnp.float32) + (BLK_SIDE * 0.5 - HALF_IMG)
    centre = x * cos + y * sin
    first = (centre + (RAYS * 0.5 - LEAD)).astype(jnp.int32)
    beta = centre + (RAYS * 0.5 - 0.5) - first.astype(jnp.float32)
    return first, beta


def fill_offsets(l_ref, subset):
    lane = lax.broadcasted_iota(jnp.int32, (8, 128), 1)
    for a, (cos, sin) in enumerate(angle_consts(subset)):
        for c in range(8):
            v = lane + c * 128
            dx = (v & 31).astype(jnp.float32) - 15.5
            dy = (v >> 5).astype(jnp.float32) - 15.5
            l_ref[a * 8 + c] = (dx * cos + dy * sin) * (1.0 / SPREAD)


def make_footprint(f_ref, l_ref, place_ref, b, subset):
    sub = lax.broadcasted_iota(jnp.int32, (8, 128), 0).astype(jnp.float32) * (1.0 / SPREAD)
    zero = jnp.zeros((8, 128), jnp.float32)
    firsts = []
    for a, (cos, sin) in enumerate(angle_consts(subset)):
        first, beta = place_of(place_ref, b, cos, sin)
        firsts.append(first)
        beta = beta * (1.0 / SPREAD)
        rays = [sub + (8 * r / SPREAD - beta) for r in range(WIN // 8)]
        for c in range(8):
            offs = l_ref[a * 8 + c]
            for t in range(WIN // 16):
                halves = []
                for r in (2 * t, 2 * t + 1):
                    if touched(cos, sin, 8 * r, c):
                        d = offs - rays[r]
                        m = jnp.maximum(1.0 - d * d, 0.0)
                        halves.append(m * m)
                    else:
                        halves.append(None)
                if halves[0] is None and halves[1] is None:
                    continue
                tile = jnp.concatenate([zero if h is None else h for h in halves], axis=0)
                f_ref[pl.ds(a * WIN + 16 * t, 16), pl.ds(c * 128, 128)] = tile.astype(jnp.bfloat16)
    return firsts


def zero_fill(f_ref):
    for r in range(KALL // 16):
        f_ref[pl.ds(16 * r, 16), :] = jnp.zeros((16, VOX), jnp.bfloat16)


def lanes(rows=8):
    return lax.broadcasted_iota(jnp.int32, (rows, 128), 1)


def project(x, f_ref):
    row = lax.broadcasted_iota(jnp.int32, (8, VOX), 0)
    ones = jnp.where(row == 0, 1.0, 0.0)
    both = jnp.concatenate([x, ones], axis=0).astype(jnp.bfloat16)
    return lax.dot_general(
        both, f_ref[...], (((1,), (1,)), ((), ())), preferred_element_type=jnp.float32
    )


def scatter_windows(acc_ref, contrib, firsts):
    lane = lanes(16)
    for a in range(ANG_SUB):
        at = a * WIN
        t0, lo = at // 128, at % 128
        piece = contrib[:, t0 * 128 : t0 * 128 + 128]
        if lo + WIN > 128:
            after = contrib[:, t0 * 128 + 128 : t0 * 128 + 256]
            piece = jnp.where(lane >= lo, piece, jnp.where(lane < lo + WIN - 128, after, 0.0))
        else:
            piece = jnp.where((lane >= lo) & (lane < lo + WIN), piece, 0.0)
        first = firsts[a]
        r = first & 127
        base = pl.multiple_of(first - r, 128)
        turned = pltpu.roll(piece, (r - lo + 128) & 127, 1)
        acc_ref[a, :, pl.ds(base, 128)] += jnp.where(lane >= r, turned, 0.0)
        acc_ref[a, :, pl.ds(base + 128, 128)] += jnp.where(lane < r, turned, 0.0)


def gather_windows(res_ref, firsts):
    lane = lanes(8)
    tiles = [jnp.zeros((8, 128), jnp.float32) for _ in range(KALL // 128)]
    for a in range(ANG_SUB):
        at = a * WIN
        t0, lo = at // 128, at % 128
        first = firsts[a]
        r = first & 127
        base = pl.multiple_of(first - r, 128)
        here = res_ref[a, :, pl.ds(base, 128)]
        after = res_ref[a, :, pl.ds(base + 128, 128)]
        turned = pltpu.roll(jnp.where(lane >= r, here, after), (lo - r + 128) & 127, 1)
        if lo + WIN > 128:
            tiles[t0] = jnp.where(lane >= lo, turned, tiles[t0])
            tiles[t0 + 1] = jnp.where(lane < lo + WIN - 128, turned, tiles[t0 + 1])
        else:
            tiles[t0] = jnp.where((lane >= lo) & (lane < lo + WIN), turned, tiles[t0])
    whole = jnp.concatenate(tiles, axis=1)
    row = lax.broadcasted_iota(jnp.int32, (8, KALL), 0)
    return jnp.concatenate([whole, jnp.where(row == 0, 1.0, 0.0)], axis=0).astype(jnp.bfloat16)


def chunk_at(a, c):
    return (c % 8) * 16 + a * 2 + c // 8


def write_chunks(out_ref, acc_ref):
    lane4 = lanes(4)
    for a in range(ANG_SUB):
        for m in range(CHUNKS // 2):
            for odd in range(2):
                whole = acc_ref[a, :, pl.ds((3 * m + 2 * odd) * 128, 128)]
                half = acc_ref[a, :, pl.ds((3 * m + 1) * 128, 128)]
                turned = pltpu.roll(half, 64, 1)
                if odd:
                    half, turned = turned, half
                packed = jnp.where(lane4 < 64, half[0:4], turned[4:8])
                sums = jnp.where(lanes(1) < 64, half[8:9], turned[8:9])
                d = chunk_at(a, 2 * m + odd)
                out_ref[d, 0:8, :] = whole[0:8]
                out_ref[d, 8:12, :] = packed
                out_ref[d, 12:13, :] = whole[8:9]
                out_ref[d, 13:14, :] = sums
                out_ref[d, 14:16, :] = jnp.zeros((2, 128), jnp.float32)


def read_chunks(res_ref, got_ref):
    lane = lanes(8)
    for a in range(ANG_SUB):
        for m in range(CHUNKS // 2):
            even = got_ref[chunk_at(a, 2 * m)].astype(jnp.float32)
            odd = got_ref[chunk_at(a, 2 * m + 1)].astype(jnp.float32)
            res_ref[a, :, pl.ds(3 * m * 128, 128)] = even[0:8]
            res_ref[a, :, pl.ds((3 * m + 2) * 128, 128)] = odd[0:8]
            he = jnp.concatenate([even[8:12], pltpu.roll(even[8:16], 64, 1)[0:4]], axis=0)
            ho = jnp.concatenate([pltpu.roll(odd[8:16], 64, 1)[0:4], odd[8:12]], axis=0)
            res_ref[a, :, pl.ds((3 * m + 1) * 128, 128)] = jnp.where(lane < 64, he, ho)
        res_ref[a, :, pl.ds(RAYS, 128)] = jnp.zeros((8, 128), jnp.float32)


def first_kernel(place_ref, x_ref, out_ref, f0, f1, l_ref, acc_ref):
    fill_offsets(l_ref, 0)
    zero_fill(f0)
    zero_fill(f1)
    acc_ref[...] = jnp.zeros_like(acc_ref)

    def step(i, carry):
        for k, f in enumerate((f0, f1)):
            b = 2 * i + k
            firsts = make_footprint(f, l_ref, place_ref, b, 0)
            scatter_windows(acc_ref, project(x_ref[b], f), firsts)
        return carry

    lax.fori_loop(0, LOCAL // 2, step, 0)
    write_chunks(out_ref, acc_ref)


def updated(x, total):
    return jnp.maximum(x + total[0:8] * (RELAX / total[8:9]), 0.0)


def middle_kernel(place_ref, got_ref, x_ref, new_ref, out_ref, f0, f1, l0, l1, acc_ref, res_ref):
    fill_offsets(l0, 0)
    fill_offsets(l1, 1)
    zero_fill(f0)
    zero_fill(f1)
    read_chunks(res_ref, got_ref)
    acc_ref[...] = jnp.zeros_like(acc_ref)

    def step(b, carry):
        firsts = make_footprint(f0, l0, place_ref, b, 0)
        total = jnp.dot(gather_windows(res_ref, firsts), f0[...], preferred_element_type=jnp.float32)
        x = updated(x_ref[b], total)
        new_ref[b] = x
        firsts = make_footprint(f1, l1, place_ref, b, 1)
        scatter_windows(acc_ref, project(x, f1), firsts)
        return carry

    lax.fori_loop(0, LOCAL, step, 0)
    write_chunks(out_ref, acc_ref)


def last_kernel(place_ref, got_ref, x_ref, new_ref, f0, f1, l_ref, res_ref):
    fill_offsets(l_ref, 1)
    zero_fill(f0)
    zero_fill(f1)
    read_chunks(res_ref, got_ref)

    def step(i, carry):
        for k, f in enumerate((f0, f1)):
            b = 2 * i + k
            firsts = make_footprint(f, l_ref, place_ref, b, 1)
            total = jnp.dot(
                gather_windows(res_ref, firsts), f[...], preferred_element_type=jnp.float32
            )
            new_ref[b] = updated(x_ref[b], total)
        return carry

    lax.fori_loop(0, LOCAL // 2, step, 0)


def residual_kernel(got_ref, meas_ref, live_ref, res_ref, send_ref):
    count = got_ref.shape[0]

    def add(i, totals):
        return tuple(t + got_ref[4 * i + k] for k, t in enumerate(totals))

    zero = jnp.zeros((16, 128), jnp.float32)
    parts = lax.fori_loop(0, count // 4, add, (zero,) * 4, unroll=4)
    total = (parts[0] + parts[1]) + (parts[2] + parts[3])
    row = lax.broadcasted_iota(jnp.int32, (16, 128), 0)
    sums = jnp.where(row < 8, total[12:13], total[13:14])
    differ = (meas_ref[...] - total / jnp.maximum(sums, 1.0)) * live_ref[...]
    res_ref[...] = differ
    rounded = differ.astype(jnp.bfloat16)

    def put(i, carry):
        send_ref[i] = rounded
        return carry

    lax.fori_loop(0, count, put, 0, unroll=8)


VM = pl.BlockSpec(memory_space=pltpu.VMEM)
SM = pl.BlockSpec(memory_space=pltpu.SMEM)
F_BUF = pltpu.VMEM((KALL, VOX), jnp.bfloat16)
L_BUF = pltpu.VMEM((ANG_SUB * 8, 8, 128), jnp.float32)
ACC_BUF = pltpu.VMEM((ANG_SUB, 16, RAYS + 128), jnp.float32)
RES_BUF = pltpu.VMEM((ANG_SUB, 8, RAYS + 128), jnp.float32)
PARAMS = pltpu.CompilerParams(vmem_limit_bytes=48 * 1024 * 1024)


def shape(dims, dtype=jnp.float32):
    return jax.ShapeDtypeStruct(dims, dtype)


def packed_rays(x, odd):
    whole = jnp.where(odd, x[:, 64:192], x[:, 0:128])
    half = jnp.where(odd, x[:, 0:64], x[:, 128:192])
    return jnp.concatenate(
        [whole, jnp.concatenate([half[0:4], half[4:8]], axis=1), jnp.zeros((4, 128), x.dtype)], axis=0
    )


def unpacked_rays(chunk, odd):
    whole = chunk[0:8]
    half = jnp.concatenate([chunk[8:12, 0:64], chunk[8:12, 64:128]], axis=0)
    return jnp.where(
        odd, jnp.concatenate([half, whole], axis=1), jnp.concatenate([whole, half], axis=1)
    )


def shards(volume, block_place, measured, live_rays):
    axes = ("group", "patch")
    group = lax.axis_index("group")
    patch = lax.axis_index("patch")
    count = lax.axis_size("group") * lax.axis_size("patch")
    odd = group % 2 == 1
    own = ANG_SUB * NTILE // count

    def masks(subset):
        rows = lax.dynamic_slice_in_dim(measured[subset], group * own, own, 0)
        rows = rows.reshape(own * RAYS_TILE, NSL).T
        live = lax.dynamic_slice_in_dim(
            live_rays[subset], (patch * lax.axis_size("group") + group) * own, own, 0
        )
        live = (jnp.arange(RAYS_TILE, dtype=jnp.int32)[None, :] < live[:, None]).astype(jnp.float32)
        live = jnp.broadcast_to(live.reshape(1, -1), (NSL, own * RAYS_TILE))
        return packed_rays(rows, odd), packed_rays(live, odd)

    def exchanged(sent):
        return lax.all_to_all(sent, axes, 0, 0, tiled=True)

    def residual(sent, subset):
        meas, live = masks(subset)
        return pl.pallas_call(
            residual_kernel,
            out_shape=(shape((16, 128)), shape((count, 16, 128), jnp.bfloat16)),
            in_specs=[VM] * 3,
            out_specs=(VM, VM),
            compiler_params=PARAMS,
        )(exchanged(sent), meas, live)

    sent = pl.pallas_call(
        first_kernel,
        out_shape=shape((count, 16, 128)),
        in_specs=[SM, VM],
        out_specs=VM,
        scratch_shapes=[F_BUF, F_BUF, L_BUF, ACC_BUF],
        compiler_params=PARAMS,
    )(block_place, volume)
    _, rounded = residual(sent, 0)
    estimate, sent = pl.pallas_call(
        middle_kernel,
        out_shape=(shape(volume.shape), shape((count, 16, 128))),
        in_specs=[SM, VM, VM],
        out_specs=(VM, VM),
        scratch_shapes=[F_BUF, F_BUF, L_BUF, L_BUF, ACC_BUF, RES_BUF],
        compiler_params=PARAMS,
    )(block_place, exchanged(rounded), volume)
    last, rounded = residual(sent, 1)
    final = pl.pallas_call(
        last_kernel,
        out_shape=shape(volume.shape),
        in_specs=[SM, VM, VM],
        out_specs=VM,
        scratch_shapes=[F_BUF, F_BUF, L_BUF, RES_BUF],
        compiler_params=PARAMS,
    )(block_place, exchanged(rounded), estimate)
    last = unpacked_rays(last, odd).T.reshape(1, own, RAYS_TILE * NSL)
    return final, last


def solution(mesh):
    return jax.shard_map(
        shards,
        mesh=mesh,
        in_specs=(
            P(("group", "patch"), None, None),
            P(("group", "patch")),
            P(None, "patch", None),
            P(),
        ),
        out_specs=(P(("group", "patch"), None, None), P("group", "patch", None)),
        check_vma=False,
    )
```

```python
import functools
import math

import jax
import jax.numpy as jnp
import numpy as np
from jax import lax
from jax.experimental import pallas as pl
from jax.experimental.pallas import tpu as pltpu
from jax.sharding import PartitionSpec as P

IMG_BLK = 64
BLK_SIDE = 32
VOX = BLK_SIDE * BLK_SIDE
RAYS_TILE = 48
NTILE = 64
ANG_SUB = 8
SUBSETS = 2
NSL = 8
SPREAD = 1.5
RELAX = 0.9
RAYS = NTILE * RAYS_TILE
WIN = 48
KALL = ANG_SUB * WIN
HALF_IMG = IMG_BLK * BLK_SIDE * 0.5
CHUNKS = 16
LOCAL = 32
DEPTH = 12
TOGETHER = 4
LEAD = 23.75


def angle_consts(subset):
    out = []
    for a in range(ANG_SUB):
        theta = np.float32(math.pi * (a * SUBSETS + subset) / (ANG_SUB * SUBSETS))
        out.append((float(np.cos(theta)), float(np.sin(theta))))
    return out


def touched(cos, sin, ray0, chunk):
    v = np.arange(chunk * 128, chunk * 128 + 128)
    along = (v % BLK_SIDE - 15.5) * cos + (v // BLK_SIDE - 15.5) * sin
    low = along.min() + LEAD - 0.5 - SPREAD - 0.01
    high = along.max() + LEAD + 0.5 + SPREAD + 0.01
    return ray0 <= high and ray0 + 7 >= low


def place_of(place_ref, b, cos, sin):
    q = place_ref[b]
    x = ((q & (IMG_BLK - 1)) * BLK_SIDE).astype(jnp.float32) + (BLK_SIDE * 0.5 - HALF_IMG)
    y = ((q >> 6) * BLK_SIDE).astype(jnp.float32) + (BLK_SIDE * 0.5 - HALF_IMG)
    centre = x * cos + y * sin
    first = (centre + (RAYS * 0.5 - LEAD)).astype(jnp.int32)
    beta = centre + (RAYS * 0.5 - 0.5) - first.astype(jnp.float32)
    return first, beta


def fill_offsets(l_ref, subset):
    lane = lax.broadcasted_iota(jnp.int32, (8, 128), 1)
    for a, (cos, sin) in enumerate(angle_consts(subset)):
        for c in range(8):
            v = lane + c * 128
            dx = (v & 31).astype(jnp.float32) - 15.5
            dy = (v >> 5).astype(jnp.float32) - 15.5
            l_ref[a * 8 + c] = (dx * cos + dy * sin) * (1.0 / SPREAD)


def windows(place_ref, b, subset):
    return [place_of(place_ref, b, cos, sin) for cos, sin in angle_consts(subset)]


def make_footprint(f_ref, l_ref, at, subset, part):
    sub = lax.broadcasted_iota(jnp.int32, (8, 128), 0).astype(jnp.float32) * (1.0 / SPREAD)
    zero = jnp.zeros((8, 128), jnp.float32)
    for a, (cos, sin) in enumerate(angle_consts(subset)):
        beta = at[a][1] * (1.0 / SPREAD)
        rays = [sub + (8 * r / SPREAD - beta) for r in range(WIN // 8)]
        for c in (2 * part, 2 * part + 1):
            offs = l_ref[a * 8 + c]
            for t in range(WIN // 16):
                halves = []
                for r in (2 * t, 2 * t + 1):
                    if touched(cos, sin, 8 * r, c):
                        d = offs - rays[r]
                        m = jnp.maximum(1.0 - d * d, 0.0)
                        halves.append(m * m)
                    else:
                        halves.append(None)
                if halves[0] is None and halves[1] is None:
                    continue
                tile = jnp.concatenate([zero if h is None else h for h in halves], axis=0)
                f_ref[pl.ds(a * WIN + 16 * t, 16), pl.ds(c * 128, 128)] = tile.astype(jnp.bfloat16)


def zero_fill(f_ref):
    for r in range(KALL // 16):
        f_ref[pl.ds(16 * r, 16), :] = jnp.zeros((16, VOX), jnp.bfloat16)


def lanes(rows=8):
    return lax.broadcasted_iota(jnp.int32, (rows, 128), 1)


def with_ones(x):
    row = lax.broadcasted_iota(jnp.int32, x.shape, 0)
    return jnp.concatenate([x, jnp.where(row == 0, 1.0, 0.0)], axis=0).astype(jnp.bfloat16)


def project(x, f_ref, cols=slice(None)):
    return lax.dot_general(
        x[:, cols], f_ref[:, cols], (((1,), (1,)), ((), ())), preferred_element_type=jnp.float32
    )


def scatter_windows(acc_ref, contrib, at):
    lane = lanes(16)
    for a in range(ANG_SUB):
        t0, lo = a * WIN // 128, a * WIN % 128
        piece = contrib[:, t0 * 128 : t0 * 128 + 128]
        if lo + WIN > 128:
            after = contrib[:, t0 * 128 + 128 : t0 * 128 + 256]
            piece = jnp.where(lane >= lo, piece, jnp.where(lane < lo + WIN - 128, after, 0.0))
        else:
            piece = jnp.where((lane >= lo) & (lane < lo + WIN), piece, 0.0)
        first = at[a][0]
        r = first & 127
        base = pl.multiple_of(first - r, 128)
        turned = pltpu.roll(piece, (r - lo + 128) & 127, 1)
        acc_ref[a, :, pl.ds(base, 128)] += jnp.where(lane >= r, turned, 0.0)
        acc_ref[a, :, pl.ds(base + 128, 128)] += jnp.where(lane < r, turned, 0.0)


def gather_windows(res_ref, at):
    lane = lanes(8)
    tiles = [jnp.zeros((8, 128), jnp.float32) for _ in range(KALL // 128)]
    for a in range(ANG_SUB):
        t0, lo = a * WIN // 128, a * WIN % 128
        first = at[a][0]
        r = first & 127
        base = pl.multiple_of(first - r, 128)
        here = res_ref[a, :, pl.ds(base, 128)]
        after = res_ref[a, :, pl.ds(base + 128, 128)]
        turned = pltpu.roll(jnp.where(lane >= r, here, after), (lo - r + 128) & 127, 1)
        if lo + WIN > 128:
            tiles[t0] = jnp.where(lane >= lo, turned, tiles[t0])
            tiles[t0 + 1] = jnp.where(lane < lo + WIN - 128, turned, tiles[t0 + 1])
        else:
            tiles[t0] = jnp.where((lane >= lo) & (lane < lo + WIN), turned, tiles[t0])
    return with_ones(jnp.concatenate(tiles, axis=1))


def chunk_at(a, c):
    return (c % 8) * 16 + a * 2 + c // 8


def write_chunks(out_ref, acc_ref):
    lane4 = lanes(4)
    for a in range(ANG_SUB):
        for m in range(CHUNKS // 2):
            for odd in range(2):
                whole = acc_ref[a, :, pl.ds((3 * m + 2 * odd) * 128, 128)]
                half = acc_ref[a, :, pl.ds((3 * m + 1) * 128, 128)]
                turned = pltpu.roll(half, 64, 1)
                if odd:
                    half, turned = turned, half
                packed = jnp.where(lane4 < 64, half[0:4], turned[4:8])
                sums = jnp.where(lanes(1) < 64, half[8:9], turned[8:9])
                d = chunk_at(a, 2 * m + odd)
                out_ref[d, 0:8, :] = whole[0:8]
                out_ref[d, 8:12, :] = packed
                out_ref[d, 12:13, :] = whole[8:9]
                out_ref[d, 13:14, :] = sums
                out_ref[d, 14:16, :] = jnp.zeros((2, 128), jnp.float32)


def read_chunks(res_ref, got_ref):
    lane = lanes(8)
    for a in range(ANG_SUB):
        for m in range(CHUNKS // 2):
            even = got_ref[chunk_at(a, 2 * m)].astype(jnp.float32)
            odd = got_ref[chunk_at(a, 2 * m + 1)].astype(jnp.float32)
            res_ref[a, :, pl.ds(3 * m * 128, 128)] = even[0:8]
            res_ref[a, :, pl.ds((3 * m + 2) * 128, 128)] = odd[0:8]
            he = jnp.concatenate([even[8:12], pltpu.roll(even[8:16], 64, 1)[0:4]], axis=0)
            ho = jnp.concatenate([pltpu.roll(odd[8:16], 64, 1)[0:4], odd[8:12]], axis=0)
            res_ref[a, :, pl.ds((3 * m + 1) * 128, 128)] = jnp.where(lane < 64, he, ho)
        res_ref[a, :, pl.ds(RAYS, 128)] = jnp.zeros((8, 128), jnp.float32)


def two_slots(step, f0, f1, make):
    for part in range(4):
        make(f0, 0)(part)

    def both(i, carry):
        step(2 * i, f0, make(f1, 2 * i + 1))
        step(2 * i + 1, f1, make(f0, jnp.minimum(2 * i + 2, LOCAL - 1)))
        return carry

    lax.fori_loop(0, LOCAL // 2, both, 0)


def first_kernel(place_ref, x_ref, out_ref, f0, f1, l_ref, acc_ref):
    fill_offsets(l_ref, 0)
    zero_fill(f0)
    zero_fill(f1)
    acc_ref[...] = jnp.zeros_like(acc_ref)

    def make(f, b):
        at = windows(place_ref, b, 0)
        return lambda part: make_footprint(f, l_ref, at, 0, part)

    def step(b, f, fill):
        x = with_ones(x_ref[b])
        contrib = 0.0
        for part in range(4):
            contrib = contrib + project(x, f, slice(part * 256, part * 256 + 256))
            fill(part)
        scatter_windows(acc_ref, contrib, windows(place_ref, b, 0))

    two_slots(step, f0, f1, make)
    write_chunks(out_ref, acc_ref)


def updated(x, total):
    return jnp.maximum(x + total[0:8] * (RELAX / total[8:9]), 0.0)


def footprint_kernel(subset, place_ref, out_ref, token_ref, slots, l_ref, sems):
    depth = slots.shape[0]
    token_ref[...] = jnp.zeros_like(token_ref)
    fill_offsets(l_ref, subset)
    for k in range(depth):
        zero_fill(slots.at[k])

    def step(b, carry):
        k = lax.rem(b, depth)

        @pl.when(b >= depth)
        def _():
            pltpu.make_async_copy(slots.at[k], out_ref.at[b - depth], sems.at[k]).wait()

        at = windows(place_ref, b, subset)
        for part in range(4):
            make_footprint(slots.at[k], l_ref, at, subset, part)
        pltpu.make_async_copy(slots.at[k], out_ref.at[b], sems.at[k]).start()
        return carry

    lax.fori_loop(0, LOCAL, step, 0)
    for k in range(depth):
        b = LOCAL - depth + k
        pltpu.make_async_copy(slots.at[b % depth], out_ref.at[b], sems.at[b % depth]).wait()


def streamed(sources, slots, sems, before, step):
    many = range(len(sources))

    def copy(n, b):
        k = lax.rem(b, DEPTH)
        return pltpu.make_async_copy(sources[n].at[b], slots[n].at[k], sems.at[n, k])

    for b in range(DEPTH - TOGETHER):
        for n in many:
            copy(n, b).start()
    before()

    def some(i, carry):
        first = i * TOGETHER

        @pl.when(first + DEPTH - TOGETHER < LOCAL)
        def _():
            for k in range(TOGETHER):
                for n in many:
                    copy(n, first + DEPTH - TOGETHER + k).start()

        for k in range(TOGETHER):
            for n in many:
                copy(n, first + k).wait()
        for k in range(TOGETHER):
            b = first + k
            step(b, [slots[n].at[lax.rem(b, DEPTH)] for n in many])
        return carry

    lax.fori_loop(0, LOCAL // TOGETHER, some, 0)


def middle_kernel(
    place_ref, got_ref, x_ref, fa, fb, new_ref, out_ref, a_slots, b_slots, acc_ref, res_ref, sems
):
    def before():
        read_chunks(res_ref, got_ref)
        acc_ref[...] = jnp.zeros_like(acc_ref)

    def step(b, refs):
        res = gather_windows(res_ref, windows(place_ref, b, 0))
        total = jnp.dot(res, refs[0][...], preferred_element_type=jnp.float32)
        x = updated(x_ref[b], total)
        new_ref[b] = x
        x = with_ones(x)
        scatter_windows(acc_ref, project(x, refs[1]), windows(place_ref, b, 1))

    streamed((fa, fb), (a_slots, b_slots), sems, before, step)
    write_chunks(out_ref, acc_ref)


def last_kernel(place_ref, got_ref, x_ref, fb, new_ref, slots, res_ref, sems):
    def before():
        read_chunks(res_ref, got_ref)

    def step(b, refs):
        res = gather_windows(res_ref, windows(place_ref, b, 1))
        total = jnp.dot(res, refs[0][...], preferred_element_type=jnp.float32)
        new_ref[b] = updated(x_ref[b], total)

    streamed((fb,), (slots,), sems, before, step)


def residual_kernel(got_ref, meas_ref, live_ref, *refs):
    res_ref, send_ref = refs[-2:]
    count = got_ref.shape[0]

    def add(i, totals):
        return tuple(t + got_ref[4 * i + k] for k, t in enumerate(totals))

    zero = jnp.zeros((16, 128), jnp.float32)
    parts = lax.fori_loop(0, count // 4, add, (zero,) * 4, unroll=4)
    total = (parts[0] + parts[1]) + (parts[2] + parts[3])
    row = lax.broadcasted_iota(jnp.int32, (16, 128), 0)
    sums = jnp.where(row < 8, total[12:13], total[13:14])
    differ = (meas_ref[...] - total / jnp.maximum(sums, 1.0)) * live_ref[...]
    res_ref[...] = differ
    rounded = differ.astype(jnp.bfloat16)

    def put(i, carry):
        send_ref[i] = rounded
        return carry

    lax.fori_loop(0, count, put, 0, unroll=8)


VM = pl.BlockSpec(memory_space=pltpu.VMEM)
ANY = pl.BlockSpec(memory_space=pl.ANY)
SM = pl.BlockSpec(memory_space=pltpu.SMEM)
F_RING = pltpu.VMEM((DEPTH, KALL, VOX), jnp.bfloat16)
F_BUF = pltpu.VMEM((KALL, VOX), jnp.bfloat16)
L_BUF = pltpu.VMEM((ANG_SUB * 8, 8, 128), jnp.float32)
ACC_BUF = pltpu.VMEM((ANG_SUB, 16, RAYS + 128), jnp.float32)
RES_BUF = pltpu.VMEM((ANG_SUB, 8, RAYS + 128), jnp.float32)
PARAMS = pltpu.CompilerParams(vmem_limit_bytes=48 * 1024 * 1024)


def shape(dims, dtype=jnp.float32):
    return jax.ShapeDtypeStruct(dims, dtype)


def packed_rays(x, odd):
    whole = jnp.where(odd, x[:, 64:192], x[:, 0:128])
    half = jnp.where(odd, x[:, 0:64], x[:, 128:192])
    return jnp.concatenate(
        [whole, jnp.concatenate([half[0:4], half[4:8]], axis=1), jnp.zeros((4, 128), x.dtype)], axis=0
    )


def unpacked_rays(chunk, odd):
    whole = chunk[0:8]
    half = jnp.concatenate([chunk[8:12, 0:64], chunk[8:12, 64:128]], axis=0)
    return jnp.where(
        odd, jnp.concatenate([half, whole], axis=1), jnp.concatenate([whole, half], axis=1)
    )


def shards(volume, block_place, measured, live_rays):
    axes = ("group", "patch")
    group = lax.axis_index("group")
    patch = lax.axis_index("patch")
    count = lax.axis_size("group") * lax.axis_size("patch")
    odd = group % 2 == 1
    own = ANG_SUB * NTILE // count

    def masks(subset):
        rows = lax.dynamic_slice_in_dim(measured[subset], group * own, own, 0)
        rows = rows.reshape(own * RAYS_TILE, NSL).T
        live = lax.dynamic_slice_in_dim(
            live_rays[subset], (patch * lax.axis_size("group") + group) * own, own, 0
        )
        live = (jnp.arange(RAYS_TILE, dtype=jnp.int32)[None, :] < live[:, None]).astype(jnp.float32)
        live = jnp.broadcast_to(live.reshape(1, -1), (NSL, own * RAYS_TILE))
        return packed_rays(rows, odd), packed_rays(live, odd)

    def exchanged(sent):
        return lax.all_to_all(sent, axes, 0, 0, tiled=True)

    def residual(sent, subset, *ready):
        meas, live = masks(subset)
        return pl.pallas_call(
            residual_kernel,
            out_shape=(shape((16, 128)), shape((count, 16, 128), jnp.bfloat16)),
            in_specs=[VM] * (3 + len(ready)),
            out_specs=(VM, VM),
            compiler_params=PARAMS,
        )(exchanged(sent), meas, live, *ready)

    sent = pl.pallas_call(
        first_kernel,
        out_shape=shape((count, 16, 128)),
        in_specs=[SM, VM],
        out_specs=VM,
        scratch_shapes=[F_BUF, F_BUF, L_BUF, ACC_BUF],
        compiler_params=PARAMS,
    )(block_place, volume)
    def footprints(subset):
        return pl.pallas_call(
            functools.partial(footprint_kernel, subset),
            out_shape=(shape((LOCAL, KALL, VOX), jnp.bfloat16), shape((8, 128))),
            in_specs=[SM],
            out_specs=(ANY, VM),
            scratch_shapes=[F_RING, L_BUF, pltpu.SemaphoreType.DMA((DEPTH,))],
            compiler_params=PARAMS,
            cost_estimate=pl.CostEstimate(
                flops=0, bytes_accessed=LOCAL * KALL * VOX * 2, transcendentals=0
            ),
        )(block_place)

    fa, token = footprints(0)
    _, rounded = residual(sent, 0, token)
    fb, _ = footprints(1)
    estimate, sent = pl.pallas_call(
        middle_kernel,
        out_shape=(shape(volume.shape), shape((count, 16, 128))),
        in_specs=[SM, VM, VM, ANY, ANY],
        out_specs=(VM, VM),
        scratch_shapes=[F_RING, F_RING, ACC_BUF, RES_BUF, pltpu.SemaphoreType.DMA((2, DEPTH))],
        compiler_params=PARAMS,
    )(block_place, exchanged(rounded), volume, fa, fb)
    last, rounded = residual(sent, 1)
    final = pl.pallas_call(
        last_kernel,
        out_shape=shape(volume.shape),
        in_specs=[SM, VM, VM, ANY],
        out_specs=VM,
        scratch_shapes=[F_RING, RES_BUF, pltpu.SemaphoreType.DMA((1, DEPTH))],
        compiler_params=PARAMS,
    )(block_place, exchanged(rounded), estimate, fb)
    last = unpacked_rays(last, odd).T.reshape(1, own, RAYS_TILE * NSL)
    return final, last


def solution(mesh):
    return jax.shard_map(
        shards,
        mesh=mesh,
        in_specs=(
            P(("group", "patch"), None, None),
            P(("group", "patch")),
            P(None, "patch", None),
            P(),
        ),
        out_specs=(P(("group", "patch"), None, None), P("group", "patch", None)),
        check_vma=False,
    )
```

```python
import functools
import math

import jax
import jax.numpy as jnp
import numpy as np
from jax import lax
from jax.experimental import pallas as pl
from jax.experimental.pallas import tpu as pltpu
from jax.sharding import PartitionSpec as P

IMG_BLK = 64
BLK_SIDE = 32
VOX = BLK_SIDE * BLK_SIDE
RAYS_TILE = 48
NTILE = 64
ANG_SUB = 8
SUBSETS = 2
NSL = 8
SPREAD = 1.5
RELAX = 0.9
RAYS = NTILE * RAYS_TILE
WIN = 48
KALL = ANG_SUB * WIN
HALF_IMG = IMG_BLK * BLK_SIDE * 0.5
CHUNKS = 16
LOCAL = 32
DEPTH = 12
MADE = 8
TOGETHER = 4
CODES = 32766.0
LEAD = 23.75


def angle_consts(subset):
    out = []
    for a in range(ANG_SUB):
        theta = np.float32(math.pi * (a * SUBSETS + subset) / (ANG_SUB * SUBSETS))
        out.append((float(np.cos(theta)), float(np.sin(theta))))
    return out


def touched(cos, sin, ray0, chunk):
    v = np.arange(chunk * 128, chunk * 128 + 128)
    along = (v % BLK_SIDE - 15.5) * cos + (v // BLK_SIDE - 15.5) * sin
    low = along.min() + LEAD - 0.5 - SPREAD - 0.01
    high = along.max() + LEAD + 0.5 + SPREAD + 0.01
    return ray0 <= high and ray0 + 7 >= low


def place_of(place_ref, b, cos, sin):
    q = place_ref[b]
    x = ((q & (IMG_BLK - 1)) * BLK_SIDE).astype(jnp.float32) + (BLK_SIDE * 0.5 - HALF_IMG)
    y = ((q >> 6) * BLK_SIDE).astype(jnp.float32) + (BLK_SIDE * 0.5 - HALF_IMG)
    centre = x * cos + y * sin
    first = (centre + (RAYS * 0.5 - LEAD)).astype(jnp.int32)
    beta = centre + (RAYS * 0.5 - 0.5) - first.astype(jnp.float32)
    return first, beta


def fill_offsets(l_ref, subset):
    lane = lax.broadcasted_iota(jnp.int32, (8, 128), 1)
    for a, (cos, sin) in enumerate(angle_consts(subset)):
        for c in range(8):
            v = lane + c * 128
            dx = (v & 31).astype(jnp.float32) - 15.5
            dy = (v >> 5).astype(jnp.float32) - 15.5
            l_ref[a * 8 + c] = (dx * cos + dy * sin) * (1.0 / SPREAD)


def windows(place_ref, b, subset):
    return [place_of(place_ref, b, cos, sin) for cos, sin in angle_consts(subset)]


def make_footprint(f_ref, l_ref, at, subset, part):
    sub = lax.broadcasted_iota(jnp.int32, (8, 128), 0).astype(jnp.float32) * (1.0 / SPREAD)
    zero = jnp.zeros((8, 128), jnp.float32)
    for a, (cos, sin) in enumerate(angle_consts(subset)):
        beta = at[a][1] * (1.0 / SPREAD)
        rays = [sub + (8 * r / SPREAD - beta) for r in range(WIN // 8)]
        for c in (2 * part, 2 * part + 1):
            offs = l_ref[a * 8 + c]
            for t in range(WIN // 16):
                halves = []
                for r in (2 * t, 2 * t + 1):
                    if touched(cos, sin, 8 * r, c):
                        d = offs - rays[r]
                        m = jnp.maximum(1.0 - d * d, 0.0)
                        halves.append(m * m)
                    else:
                        halves.append(None)
                if halves[0] is None and halves[1] is None:
                    continue
                tile = jnp.concatenate([zero if h is None else h for h in halves], axis=0)
                f_ref[pl.ds(a * WIN + 16 * t, 16), pl.ds(c * 128, 128)] = tile.astype(jnp.bfloat16)


def zero_fill(f_ref):
    for r in range(KALL // 16):
        f_ref[pl.ds(16 * r, 16), :] = jnp.zeros((16, VOX), jnp.bfloat16)


def lanes(rows=8):
    return lax.broadcasted_iota(jnp.int32, (rows, 128), 1)


def with_ones(x):
    row = lax.broadcasted_iota(jnp.int32, x.shape, 0)
    return jnp.concatenate([x, jnp.where(row == 0, 1.0, 0.0)], axis=0).astype(jnp.bfloat16)


def project(x, f_ref, cols=slice(None)):
    return lax.dot_general(
        x[:, cols], f_ref[:, cols], (((1,), (1,)), ((), ())), preferred_element_type=jnp.float32
    )


def scatter_windows(acc_ref, contrib, at):
    lane = lanes(16)
    for a in range(ANG_SUB):
        t0, lo = a * WIN // 128, a * WIN % 128
        piece = contrib[:, t0 * 128 : t0 * 128 + 128]
        if lo + WIN > 128:
            after = contrib[:, t0 * 128 + 128 : t0 * 128 + 256]
            piece = jnp.where(lane >= lo, piece, jnp.where(lane < lo + WIN - 128, after, 0.0))
        else:
            piece = jnp.where((lane >= lo) & (lane < lo + WIN), piece, 0.0)
        first = at[a][0]
        r = first & 127
        base = pl.multiple_of(first - r, 128)
        turned = pltpu.roll(piece, (r - lo + 128) & 127, 1)
        acc_ref[a, :, pl.ds(base, 128)] += jnp.where(lane >= r, turned, 0.0)
        acc_ref[a, :, pl.ds(base + 128, 128)] += jnp.where(lane < r, turned, 0.0)


def gather_windows(res_ref, at):
    lane = lanes(8)
    tiles = [jnp.zeros((8, 128), jnp.float32) for _ in range(KALL // 128)]
    for a in range(ANG_SUB):
        t0, lo = a * WIN // 128, a * WIN % 128
        first = at[a][0]
        r = first & 127
        base = pl.multiple_of(first - r, 128)
        here = res_ref[a, :, pl.ds(base, 128)]
        after = res_ref[a, :, pl.ds(base + 128, 128)]
        turned = pltpu.roll(jnp.where(lane >= r, here, after), (lo - r + 128) & 127, 1)
        if lo + WIN > 128:
            tiles[t0] = jnp.where(lane >= lo, turned, tiles[t0])
            tiles[t0 + 1] = jnp.where(lane < lo + WIN - 128, turned, tiles[t0 + 1])
        else:
            tiles[t0] = jnp.where((lane >= lo) & (lane < lo + WIN), turned, tiles[t0])
    return with_ones(jnp.concatenate(tiles, axis=1))


def chunk_at(a, c):
    return (c % 8) * 16 + a * 2 + c // 8


def coded(x, unit):
    root = jnp.sqrt(jnp.sqrt(x))
    return (root * (CODES / jnp.sqrt(jnp.sqrt(unit))) + 0.5).astype(jnp.int32)


def decoded(codes, unit):
    part = codes * (1.0 / CODES)
    part = part * part
    return part * part * unit


def write_chunks(out_ref, acc_ref):
    lane4 = lanes(4)
    largest = jnp.zeros((16, 128), jnp.float32)
    for a in range(ANG_SUB):
        for t in range(RAYS // 128):
            largest = jnp.maximum(largest, acc_ref[a, :, pl.ds(t * 128, 128)])
    half_unit = jnp.floor(jnp.max(largest[0:8], axis=(0, 1), keepdims=True) * 0.5) + 1.0
    sum_unit = jnp.floor(jnp.max(largest[8:9], axis=(0, 1), keepdims=True)) + 1.0
    unit = half_unit * 2.0
    units = jnp.concatenate(
        [jnp.broadcast_to(u, (1, 128)).astype(jnp.int32) for u in (half_unit, sum_unit)], axis=0
    )
    for a in range(ANG_SUB):
        for m in range(CHUNKS // 2):
            for odd in range(2):
                whole = acc_ref[a, :, pl.ds((3 * m + 2 * odd) * 128, 128)]
                half = acc_ref[a, :, pl.ds((3 * m + 1) * 128, 128)]
                turned = pltpu.roll(half, 64, 1)
                if odd:
                    half, turned = turned, half
                packed = jnp.where(lane4 < 64, half[0:4], turned[4:8])
                sums = jnp.where(lanes(1) < 64, half[8:9], turned[8:9])
                sums = coded(jnp.concatenate([whole[8:9], sums], axis=0), sum_unit)
                chunk = jnp.concatenate(
                    [coded(whole[0:8], unit), coded(packed, unit), sums, units], axis=0
                )
                out_ref[chunk_at(a, 2 * m + odd)] = chunk.astype(jnp.int16)


def read_chunks(res_ref, got_ref):
    lane = lanes(8)
    for a in range(ANG_SUB):
        for m in range(CHUNKS // 2):
            even = got_ref[chunk_at(a, 2 * m)].astype(jnp.float32)
            odd = got_ref[chunk_at(a, 2 * m + 1)].astype(jnp.float32)
            res_ref[a, :, pl.ds(3 * m * 128, 128)] = even[0:8]
            res_ref[a, :, pl.ds((3 * m + 2) * 128, 128)] = odd[0:8]
            he = jnp.concatenate([even[8:12], pltpu.roll(even[8:16], 64, 1)[0:4]], axis=0)
            ho = jnp.concatenate([pltpu.roll(odd[8:16], 64, 1)[0:4], odd[8:12]], axis=0)
            res_ref[a, :, pl.ds((3 * m + 1) * 128, 128)] = jnp.where(lane < 64, he, ho)
        res_ref[a, :, pl.ds(RAYS, 128)] = jnp.zeros((8, 128), jnp.float32)


def two_slots(step, f0, f1, make):
    for part in range(4):
        make(f0, 0)(part)

    def both(i, carry):
        step(2 * i, f0, make(f1, 2 * i + 1))
        step(2 * i + 1, f1, make(f0, jnp.minimum(2 * i + 2, LOCAL - 1)))
        return carry

    lax.fori_loop(0, LOCAL // 2, both, 0)


def first_kernel(place_ref, x_ref, out_ref, f0, f1, l_ref, acc_ref):
    fill_offsets(l_ref, 0)
    zero_fill(f0)
    zero_fill(f1)
    acc_ref[...] = jnp.zeros_like(acc_ref)

    def make(f, b):
        at = windows(place_ref, b, 0)
        return lambda part: make_footprint(f, l_ref, at, 0, part)

    def step(b, f, fill):
        x = with_ones(x_ref[b])
        contrib = 0.0
        for part in range(4):
            contrib = contrib + project(x, f, slice(part * 256, part * 256 + 256))
            fill(part)
        scatter_windows(acc_ref, contrib, windows(place_ref, b, 0))

    two_slots(step, f0, f1, make)
    write_chunks(out_ref, acc_ref)


def updated(x, total):
    return jnp.maximum(x + total[0:8] * (RELAX / total[8:9]), 0.0)


def footprint_kernel(subset, place_ref, out_ref, token_ref, slots, l_ref, sems):
    token_ref[...] = jnp.zeros_like(token_ref)
    fill_offsets(l_ref, subset)
    for k in range(MADE):
        zero_fill(slots.at[k])

    def some(i, carry):
        for k in range(MADE):
            b = i * MADE + k

            @pl.when(i > 0)
            def _():
                pltpu.make_async_copy(slots.at[k], out_ref.at[b], sems.at[k]).wait()

            at = windows(place_ref, b, subset)
            for part in range(4):
                make_footprint(slots.at[k], l_ref, at, subset, part)
            pltpu.make_async_copy(slots.at[k], out_ref.at[b], sems.at[k]).start()
        return carry

    lax.fori_loop(0, LOCAL // MADE, some, 0)
    for k in range(MADE):
        pltpu.make_async_copy(slots.at[k], out_ref.at[LOCAL - MADE + k], sems.at[k]).wait()


def streamed(sources, slots, sems, before, step):
    many = range(len(sources))

    def copy(n, b):
        k = lax.rem(b, DEPTH)
        return pltpu.make_async_copy(sources[n].at[b], slots[n].at[k], sems.at[n, k])

    for b in range(DEPTH - TOGETHER):
        for n in many:
            copy(n, b).start()
    before()

    def some(i, carry):
        first = i * TOGETHER

        @pl.when(first + DEPTH - TOGETHER < LOCAL)
        def _():
            for k in range(TOGETHER):
                for n in many:
                    copy(n, first + DEPTH - TOGETHER + k).start()

        for k in range(TOGETHER):
            for n in many:
                copy(n, first + k).wait()
        for k in range(TOGETHER):
            b = first + k
            step(b, [slots[n].at[lax.rem(b, DEPTH)] for n in many])
        return carry

    lax.fori_loop(0, LOCAL // TOGETHER, some, 0)


def middle_kernel(
    place_ref, got_ref, x_ref, fa, fb, new_ref, out_ref, a_slots, b_slots, acc_ref, res_ref, sems
):
    def before():
        read_chunks(res_ref, got_ref)
        acc_ref[...] = jnp.zeros_like(acc_ref)

    def step(b, refs):
        res = gather_windows(res_ref, windows(place_ref, b, 0))
        total = jnp.dot(res, refs[0][...], preferred_element_type=jnp.float32)
        x = updated(x_ref[b], total)
        new_ref[b] = x
        x = with_ones(x)
        scatter_windows(acc_ref, project(x, refs[1]), windows(place_ref, b, 1))

    streamed((fa, fb), (a_slots, b_slots), sems, before, step)
    write_chunks(out_ref, acc_ref)


def last_kernel(place_ref, got_ref, x_ref, fb, new_ref, slots, res_ref, sems):
    def before():
        read_chunks(res_ref, got_ref)

    def step(b, refs):
        res = gather_windows(res_ref, windows(place_ref, b, 1))
        total = jnp.dot(res, refs[0][...], preferred_element_type=jnp.float32)
        new_ref[b] = updated(x_ref[b], total)

    streamed((fb,), (slots,), sems, before, step)


def residual_kernel(got_ref, meas_ref, live_ref, *refs):
    res_ref, send_ref = refs[-2:]
    count = got_ref.shape[0]

    row = lax.broadcasted_iota(jnp.int32, (16, 128), 0)

    def add(i, totals):
        out = []
        for k, t in enumerate(totals):
            chunk = got_ref[4 * i + k].astype(jnp.int32).astype(jnp.float32)
            unit = jnp.where(row < 12, chunk[14:15] * 2.0, chunk[15:16])
            out.append(t + decoded(chunk, unit))
        return tuple(out)

    zero = jnp.zeros((16, 128), jnp.float32)
    parts = lax.fori_loop(0, count // 4, add, (zero,) * 4, unroll=4)
    total = (parts[0] + parts[1]) + (parts[2] + parts[3])
    sums = jnp.where(row < 8, total[12:13], total[13:14])
    differ = (meas_ref[...] - total / jnp.maximum(sums, 1.0)) * live_ref[...]
    res_ref[...] = differ
    rounded = differ.astype(jnp.bfloat16)

    def put(i, carry):
        send_ref[i] = rounded
        return carry

    lax.fori_loop(0, count, put, 0, unroll=8)


VM = pl.BlockSpec(memory_space=pltpu.VMEM)
ANY = pl.BlockSpec(memory_space=pl.ANY)
SM = pl.BlockSpec(memory_space=pltpu.SMEM)
F_RING = pltpu.VMEM((DEPTH, KALL, VOX), jnp.bfloat16)
F_BUF = pltpu.VMEM((KALL, VOX), jnp.bfloat16)
L_BUF = pltpu.VMEM((ANG_SUB * 8, 8, 128), jnp.float32)
ACC_BUF = pltpu.VMEM((ANG_SUB, 16, RAYS + 128), jnp.float32)
RES_BUF = pltpu.VMEM((ANG_SUB, 8, RAYS + 128), jnp.float32)
PARAMS = pltpu.CompilerParams(vmem_limit_bytes=48 * 1024 * 1024)


def shape(dims, dtype=jnp.float32):
    return jax.ShapeDtypeStruct(dims, dtype)


def packed_rays(x, odd):
    whole = jnp.where(odd, x[:, 64:192], x[:, 0:128])
    half = jnp.where(odd, x[:, 0:64], x[:, 128:192])
    return jnp.concatenate(
        [whole, jnp.concatenate([half[0:4], half[4:8]], axis=1), jnp.zeros((4, 128), x.dtype)], axis=0
    )


def unpacked_rays(chunk, odd):
    whole = chunk[0:8]
    half = jnp.concatenate([chunk[8:12, 0:64], chunk[8:12, 64:128]], axis=0)
    return jnp.where(
        odd, jnp.concatenate([half, whole], axis=1), jnp.concatenate([whole, half], axis=1)
    )


def shards(volume, block_place, measured, live_rays):
    axes = ("group", "patch")
    group = lax.axis_index("group")
    patch = lax.axis_index("patch")
    count = lax.axis_size("group") * lax.axis_size("patch")
    odd = group % 2 == 1
    own = ANG_SUB * NTILE // count

    def masks(subset):
        rows = lax.dynamic_slice_in_dim(measured[subset], group * own, own, 0)
        rows = rows.reshape(own * RAYS_TILE, NSL).T
        live = lax.dynamic_slice_in_dim(
            live_rays[subset], (patch * lax.axis_size("group") + group) * own, own, 0
        )
        live = (jnp.arange(RAYS_TILE, dtype=jnp.int32)[None, :] < live[:, None]).astype(jnp.float32)
        live = jnp.broadcast_to(live.reshape(1, -1), (NSL, own * RAYS_TILE))
        return packed_rays(rows, odd), packed_rays(live, odd)

    def exchanged(sent):
        return lax.all_to_all(sent, axes, 0, 0, tiled=True)

    def residual(sent, subset, *ready):
        meas, live = masks(subset)
        return pl.pallas_call(
            residual_kernel,
            out_shape=(shape((16, 128)), shape((count, 16, 128), jnp.bfloat16)),
            in_specs=[VM] * (3 + len(ready)),
            out_specs=(VM, VM),
            compiler_params=PARAMS,
        )(exchanged(sent), meas, live, *ready)

    sent = pl.pallas_call(
        first_kernel,
        out_shape=shape((count, 16, 128), jnp.int16),
        in_specs=[SM, VM],
        out_specs=VM,
        scratch_shapes=[F_BUF, F_BUF, L_BUF, ACC_BUF],
        compiler_params=PARAMS,
    )(block_place, volume)
    def footprints(subset):
        return pl.pallas_call(
            functools.partial(footprint_kernel, subset),
            out_shape=(shape((LOCAL, KALL, VOX), jnp.bfloat16), shape((8, 128))),
            in_specs=[SM],
            out_specs=(ANY, VM),
            scratch_shapes=[
                pltpu.VMEM((MADE, KALL, VOX), jnp.bfloat16),
                L_BUF,
                pltpu.SemaphoreType.DMA((MADE,)),
            ],
            compiler_params=PARAMS,
            cost_estimate=pl.CostEstimate(
                flops=0, bytes_accessed=LOCAL * KALL * VOX * 2, transcendentals=0
            ),
        )(block_place)

    fa, token = footprints(0)
    _, rounded = residual(sent, 0, token)
    fb, _ = footprints(1)
    estimate, sent = pl.pallas_call(
        middle_kernel,
        out_shape=(shape(volume.shape), shape((count, 16, 128), jnp.int16)),
        in_specs=[SM, VM, VM, ANY, ANY],
        out_specs=(VM, VM),
        scratch_shapes=[F_RING, F_RING, ACC_BUF, RES_BUF, pltpu.SemaphoreType.DMA((2, DEPTH))],
        compiler_params=PARAMS,
    )(block_place, exchanged(rounded), volume, fa, fb)
    last, rounded = residual(sent, 1)
    final = pl.pallas_call(
        last_kernel,
        out_shape=shape(volume.shape),
        in_specs=[SM, VM, VM, ANY],
        out_specs=VM,
        scratch_shapes=[F_RING, RES_BUF, pltpu.SemaphoreType.DMA((1, DEPTH))],
        compiler_params=PARAMS,
    )(block_place, exchanged(rounded), estimate, fb)
    last = unpacked_rays(last, odd).T.reshape(1, own, RAYS_TILE * NSL)
    return final, last


def solution(mesh):
    return jax.shard_map(
        shards,
        mesh=mesh,
        in_specs=(
            P(("group", "patch"), None, None),
            P(("group", "patch")),
            P(None, "patch", None),
            P(),
        ),
        out_specs=(P(("group", "patch"), None, None), P("group", "patch", None)),
        check_vma=False,
    )
```

```python
import functools
import math

import jax
import jax.numpy as jnp
import numpy as np
from jax import lax
from jax.experimental import pallas as pl
from jax.experimental.pallas import tpu as pltpu
from jax.sharding import PartitionSpec as P

IMG_BLK = 64
BLK_SIDE = 32
VOX = BLK_SIDE * BLK_SIDE
RAYS_TILE = 48
NTILE = 64
ANG_SUB = 8
SUBSETS = 2
NSL = 8
SPREAD = 1.5
RELAX = 0.9
RAYS = NTILE * RAYS_TILE
WIN = 48
KALL = ANG_SUB * WIN
HALF_IMG = IMG_BLK * BLK_SIDE * 0.5
CHUNKS = 16
LOCAL = 32
DEPTH = 12
MADE = 8
TOGETHER = 4
CODES = 32766.0
LEAD = 23.75


def angle_consts(subset):
    out = []
    for a in range(ANG_SUB):
        theta = np.float32(math.pi * (a * SUBSETS + subset) / (ANG_SUB * SUBSETS))
        out.append((float(np.cos(theta)), float(np.sin(theta))))
    return out


def touched(cos, sin, ray0, chunk):
    v = np.arange(chunk * 128, chunk * 128 + 128)
    along = (v % BLK_SIDE - 15.5) * cos + (v // BLK_SIDE - 15.5) * sin
    low = along.min() + LEAD - 0.5 - SPREAD - 0.01
    high = along.max() + LEAD + 0.5 + SPREAD + 0.01
    return ray0 <= high and ray0 + 7 >= low


def place_of(place_ref, b, cos, sin):
    q = place_ref[b]
    x = ((q & (IMG_BLK - 1)) * BLK_SIDE).astype(jnp.float32) + (BLK_SIDE * 0.5 - HALF_IMG)
    y = ((q >> 6) * BLK_SIDE).astype(jnp.float32) + (BLK_SIDE * 0.5 - HALF_IMG)
    centre = x * cos + y * sin
    first = (centre + (RAYS * 0.5 - LEAD)).astype(jnp.int32)
    beta = centre + (RAYS * 0.5 - 0.5) - first.astype(jnp.float32)
    return first, beta


def fill_offsets(l_ref, subset):
    lane = lax.broadcasted_iota(jnp.int32, (8, 128), 1)
    for a, (cos, sin) in enumerate(angle_consts(subset)):
        for c in range(8):
            v = lane + c * 128
            dx = (v & 31).astype(jnp.float32) - 15.5
            dy = (v >> 5).astype(jnp.float32) - 15.5
            l_ref[a * 8 + c] = (dx * cos + dy * sin) * (1.0 / SPREAD)


def windows(place_ref, b, subset):
    return [place_of(place_ref, b, cos, sin) for cos, sin in angle_consts(subset)]


def make_footprint(f_ref, l_ref, at, subset, part):
    sub = lax.broadcasted_iota(jnp.int32, (8, 128), 0).astype(jnp.float32) * (1.0 / SPREAD)
    zero = jnp.zeros((8, 128), jnp.float32)
    for a, (cos, sin) in enumerate(angle_consts(subset)):
        beta = at[a][1] * (1.0 / SPREAD)
        rays = [sub + (8 * r / SPREAD - beta) for r in range(WIN // 8)]
        for c in (2 * part, 2 * part + 1):
            offs = l_ref[a * 8 + c]
            for t in range(WIN // 16):
                halves = []
                for r in (2 * t, 2 * t + 1):
                    if touched(cos, sin, 8 * r, c):
                        d = offs - rays[r]
                        m = jnp.maximum(1.0 - d * d, 0.0)
                        halves.append(m * m)
                    else:
                        halves.append(None)
                if halves[0] is None and halves[1] is None:
                    continue
                tile = jnp.concatenate([zero if h is None else h for h in halves], axis=0)
                f_ref[pl.ds(a * WIN + 16 * t, 16), pl.ds(c * 128, 128)] = tile.astype(jnp.bfloat16)


def zero_fill(f_ref):
    for r in range(KALL // 16):
        f_ref[pl.ds(16 * r, 16), :] = jnp.zeros((16, VOX), jnp.bfloat16)


def lanes(rows=8):
    return lax.broadcasted_iota(jnp.int32, (rows, 128), 1)


def with_ones(x):
    row = lax.broadcasted_iota(jnp.int32, x.shape, 0)
    return jnp.concatenate([x, jnp.where(row == 0, 1.0, 0.0)], axis=0).astype(jnp.bfloat16)


def project(x, f_ref, cols=slice(None)):
    return lax.dot_general(
        x[:, cols], f_ref[:, cols], (((1,), (1,)), ((), ())), preferred_element_type=jnp.float32
    )


def scatter_windows(acc_ref, contrib, at):
    lane = lanes(16)
    for a in range(ANG_SUB):
        t0, lo = a * WIN // 128, a * WIN % 128
        piece = contrib[:, t0 * 128 : t0 * 128 + 128]
        if lo + WIN > 128:
            after = contrib[:, t0 * 128 + 128 : t0 * 128 + 256]
            piece = jnp.where(lane >= lo, piece, jnp.where(lane < lo + WIN - 128, after, 0.0))
        else:
            piece = jnp.where((lane >= lo) & (lane < lo + WIN), piece, 0.0)
        first = at[a][0]
        r = first & 127
        base = pl.multiple_of(first - r, 128)
        turned = pltpu.roll(piece, (r - lo + 128) & 127, 1)
        acc_ref[a, :, pl.ds(base, 128)] += jnp.where(lane >= r, turned, 0.0)
        acc_ref[a, :, pl.ds(base + 128, 128)] += jnp.where(lane < r, turned, 0.0)


def gather_windows(res_ref, at):
    lane = lanes(8)
    tiles = [jnp.zeros((8, 128), jnp.float32) for _ in range(KALL // 128)]
    for a in range(ANG_SUB):
        t0, lo = a * WIN // 128, a * WIN % 128
        first = at[a][0]
        r = first & 127
        base = pl.multiple_of(first - r, 128)
        here = res_ref[a, :, pl.ds(base, 128)]
        after = res_ref[a, :, pl.ds(base + 128, 128)]
        turned = pltpu.roll(jnp.where(lane >= r, here, after), (lo - r + 128) & 127, 1)
        if lo + WIN > 128:
            tiles[t0] = jnp.where(lane >= lo, turned, tiles[t0])
            tiles[t0 + 1] = jnp.where(lane < lo + WIN - 128, turned, tiles[t0 + 1])
        else:
            tiles[t0] = jnp.where((lane >= lo) & (lane < lo + WIN), turned, tiles[t0])
    return with_ones(jnp.concatenate(tiles, axis=1))


def chunk_at(a, c):
    return (c % 8) * 16 + a * 2 + c // 8


def coded(x, unit):
    root = jnp.sqrt(jnp.sqrt(x))
    return (root * (CODES / jnp.sqrt(jnp.sqrt(unit))) + 0.5).astype(jnp.int32)


def decoded(codes, unit):
    part = codes * (1.0 / CODES)
    part = part * part
    return part * part * unit


def write_chunks(out_ref, acc_ref):
    lane4 = lanes(4)
    largest = jnp.zeros((16, 128), jnp.float32)
    for a in range(ANG_SUB):
        for t in range(RAYS // 128):
            largest = jnp.maximum(largest, acc_ref[a, :, pl.ds(t * 128, 128)])
    half_unit = jnp.floor(jnp.max(largest[0:8], axis=(0, 1), keepdims=True) * 0.5) + 1.0
    sum_unit = jnp.floor(jnp.max(largest[8:9], axis=(0, 1), keepdims=True)) + 1.0
    unit = half_unit * 2.0
    units = jnp.concatenate(
        [jnp.broadcast_to(u, (1, 128)).astype(jnp.int32) for u in (half_unit, sum_unit)], axis=0
    )
    for a in range(ANG_SUB):
        for m in range(CHUNKS // 2):
            for odd in range(2):
                whole = acc_ref[a, :, pl.ds((3 * m + 2 * odd) * 128, 128)]
                half = acc_ref[a, :, pl.ds((3 * m + 1) * 128, 128)]
                turned = pltpu.roll(half, 64, 1)
                if odd:
                    half, turned = turned, half
                packed = jnp.where(lane4 < 64, half[0:4], turned[4:8])
                sums = jnp.where(lanes(1) < 64, half[8:9], turned[8:9])
                sums = coded(jnp.concatenate([whole[8:9], sums], axis=0), sum_unit)
                chunk = jnp.concatenate(
                    [coded(whole[0:8], unit), coded(packed, unit), sums, units], axis=0
                )
                out_ref[chunk_at(a, 2 * m + odd)] = chunk.astype(jnp.int16)


def read_chunks(res_ref, got_ref):
    lane = lanes(8)
    for a in range(ANG_SUB):
        for m in range(CHUNKS // 2):
            even = got_ref[chunk_at(a, 2 * m)].astype(jnp.float32)
            odd = got_ref[chunk_at(a, 2 * m + 1)].astype(jnp.float32)
            res_ref[a, :, pl.ds(3 * m * 128, 128)] = even[0:8]
            res_ref[a, :, pl.ds((3 * m + 2) * 128, 128)] = odd[0:8]
            he = jnp.concatenate([even[8:12], pltpu.roll(even[8:16], 64, 1)[0:4]], axis=0)
            ho = jnp.concatenate([pltpu.roll(odd[8:16], 64, 1)[0:4], odd[8:12]], axis=0)
            res_ref[a, :, pl.ds((3 * m + 1) * 128, 128)] = jnp.where(lane < 64, he, ho)
        res_ref[a, :, pl.ds(RAYS, 128)] = jnp.zeros((8, 128), jnp.float32)


def two_slots(step, f0, f1, make):
    for part in range(4):
        make(f0, 0)(part)

    def both(i, carry):
        step(2 * i, f0, make(f1, 2 * i + 1))
        step(2 * i + 1, f1, make(f0, jnp.minimum(2 * i + 2, LOCAL - 1)))
        return carry

    lax.fori_loop(0, LOCAL // 2, both, 0)


def first_kernel(place_ref, x_ref, out_ref, f0, f1, l_ref, acc_ref):
    fill_offsets(l_ref, 0)
    zero_fill(f0)
    zero_fill(f1)
    acc_ref[...] = jnp.zeros_like(acc_ref)

    def make(f, b):
        at = windows(place_ref, b, 0)
        return lambda part: make_footprint(f, l_ref, at, 0, part)

    def step(b, f, fill):
        x = with_ones(x_ref[b])
        contrib = 0.0
        for part in range(4):
            contrib = contrib + project(x, f, slice(part * 256, part * 256 + 256))
            fill(part)
        scatter_windows(acc_ref, contrib, windows(place_ref, b, 0))

    two_slots(step, f0, f1, make)
    write_chunks(out_ref, acc_ref)


def updated(x, total):
    return jnp.maximum(x + total[0:8] * (RELAX / total[8:9]), 0.0)


def footprint_kernel(subset, start, place_ref, *refs):
    out_ref, token_ref, slots, l_ref, sems = refs[-5:]
    token_ref[...] = jnp.zeros_like(token_ref)
    fill_offsets(l_ref, subset)
    for k in range(MADE):
        zero_fill(slots.at[k])

    def some(i, carry):
        for k in range(MADE):
            b = start + i * MADE + k

            @pl.when(i > 0)
            def _():
                pltpu.make_async_copy(slots.at[k], out_ref.at[b], sems.at[k]).wait()

            at = windows(place_ref, b, subset)
            for part in range(4):
                make_footprint(slots.at[k], l_ref, at, subset, part)
            pltpu.make_async_copy(slots.at[k], out_ref.at[b], sems.at[k]).start()
        return carry

    lax.fori_loop(0, LOCAL // 2 // MADE, some, 0)
    for k in range(MADE):
        b = start + LOCAL // 2 - MADE + k
        pltpu.make_async_copy(slots.at[k], out_ref.at[b], sems.at[k]).wait()


def streamed(sources, slots, sems, before, step):
    many = range(len(sources))

    def copy(n, b):
        k = lax.rem(b, DEPTH)
        return pltpu.make_async_copy(sources[n].at[b], slots[n].at[k], sems.at[n, k])

    for b in range(DEPTH - TOGETHER):
        for n in many:
            copy(n, b).start()
    before()

    def some(i, carry):
        first = i * TOGETHER

        @pl.when(first + DEPTH - TOGETHER < LOCAL)
        def _():
            for k in range(TOGETHER):
                for n in many:
                    copy(n, first + DEPTH - TOGETHER + k).start()

        for k in range(TOGETHER):
            for n in many:
                copy(n, first + k).wait()
        for k in range(TOGETHER):
            b = first + k
            step(b, k, [slots[n].at[lax.rem(b, DEPTH)] for n in many])
        return carry

    lax.fori_loop(0, LOCAL // TOGETHER, some, 0)


def middle_kernel(
    place_ref, got_ref, x_ref, fa, new_ref, out_ref, ring, g0, g1, l_ref, acc_ref, res_ref, sems
):
    made = (g0, g1)

    def make(f, b):
        at = windows(place_ref, b, 1)
        return lambda part: make_footprint(f, l_ref, at, 1, part)

    def before():
        fill_offsets(l_ref, 1)
        zero_fill(g0)
        zero_fill(g1)
        for part in range(4):
            make(g0, 0)(part)
        read_chunks(res_ref, got_ref)
        acc_ref[...] = jnp.zeros_like(acc_ref)

    def step(b, k, refs):
        f = made[k % 2]
        fill = make(made[(k + 1) % 2], jnp.minimum(b + 1, LOCAL - 1))
        res = gather_windows(res_ref, windows(place_ref, b, 0))
        total = jnp.dot(res, refs[0][...], preferred_element_type=jnp.float32)
        x = updated(x_ref[b], total)
        new_ref[b] = x
        x = with_ones(x)
        contrib = 0.0
        for part in range(4):
            contrib = contrib + project(x, f, slice(part * 256, part * 256 + 256))
            fill(part)
        scatter_windows(acc_ref, contrib, windows(place_ref, b, 1))

    streamed((fa,), (ring,), sems, before, step)
    write_chunks(out_ref, acc_ref)


def last_kernel(place_ref, got_ref, x_ref, fb, new_ref, slots, res_ref, sems):
    def before():
        read_chunks(res_ref, got_ref)

    def step(b, k, refs):
        res = gather_windows(res_ref, windows(place_ref, b, 1))
        total = jnp.dot(res, refs[0][...], preferred_element_type=jnp.float32)
        new_ref[b] = updated(x_ref[b], total)

    streamed((fb,), (slots,), sems, before, step)


def residual_kernel(got_ref, meas_ref, live_ref, *refs):
    res_ref, send_ref = refs[-2:]
    count = got_ref.shape[0]

    row = lax.broadcasted_iota(jnp.int32, (16, 128), 0)

    def add(i, totals):
        out = []
        for k, t in enumerate(totals):
            chunk = got_ref[4 * i + k].astype(jnp.int32).astype(jnp.float32)
            unit = jnp.where(row < 12, chunk[14:15] * 2.0, chunk[15:16])
            out.append(t + decoded(chunk, unit))
        return tuple(out)

    zero = jnp.zeros((16, 128), jnp.float32)
    parts = lax.fori_loop(0, count // 4, add, (zero,) * 4, unroll=4)
    total = (parts[0] + parts[1]) + (parts[2] + parts[3])
    sums = jnp.where(row < 8, total[12:13], total[13:14])
    differ = (meas_ref[...] - total / jnp.maximum(sums, 1.0)) * live_ref[...]
    res_ref[...] = differ
    rounded = differ.astype(jnp.bfloat16)

    def put(i, carry):
        send_ref[i] = rounded
        return carry

    lax.fori_loop(0, count, put, 0, unroll=8)


VM = pl.BlockSpec(memory_space=pltpu.VMEM)
ANY = pl.BlockSpec(memory_space=pl.ANY)
SM = pl.BlockSpec(memory_space=pltpu.SMEM)
F_RING = pltpu.VMEM((DEPTH, KALL, VOX), jnp.bfloat16)
F_BUF = pltpu.VMEM((KALL, VOX), jnp.bfloat16)
L_BUF = pltpu.VMEM((ANG_SUB * 8, 8, 128), jnp.float32)
ACC_BUF = pltpu.VMEM((ANG_SUB, 16, RAYS + 128), jnp.float32)
RES_BUF = pltpu.VMEM((ANG_SUB, 8, RAYS + 128), jnp.float32)
PARAMS = pltpu.CompilerParams(vmem_limit_bytes=48 * 1024 * 1024)


def shape(dims, dtype=jnp.float32):
    return jax.ShapeDtypeStruct(dims, dtype)


def packed_rays(x, odd):
    whole = jnp.where(odd, x[:, 64:192], x[:, 0:128])
    half = jnp.where(odd, x[:, 0:64], x[:, 128:192])
    return jnp.concatenate(
        [whole, jnp.concatenate([half[0:4], half[4:8]], axis=1), jnp.zeros((4, 128), x.dtype)], axis=0
    )


def unpacked_rays(chunk, odd):
    whole = chunk[0:8]
    half = jnp.concatenate([chunk[8:12, 0:64], chunk[8:12, 64:128]], axis=0)
    return jnp.where(
        odd, jnp.concatenate([half, whole], axis=1), jnp.concatenate([whole, half], axis=1)
    )


def shards(volume, block_place, measured, live_rays):
    axes = ("group", "patch")
    group = lax.axis_index("group")
    patch = lax.axis_index("patch")
    count = lax.axis_size("group") * lax.axis_size("patch")
    odd = group % 2 == 1
    own = ANG_SUB * NTILE // count

    def masks(subset):
        rows = lax.dynamic_slice_in_dim(measured[subset], group * own, own, 0)
        rows = rows.reshape(own * RAYS_TILE, NSL).T
        live = lax.dynamic_slice_in_dim(
            live_rays[subset], (patch * lax.axis_size("group") + group) * own, own, 0
        )
        live = (jnp.arange(RAYS_TILE, dtype=jnp.int32)[None, :] < live[:, None]).astype(jnp.float32)
        live = jnp.broadcast_to(live.reshape(1, -1), (NSL, own * RAYS_TILE))
        return packed_rays(rows, odd), packed_rays(live, odd)

    def exchanged(sent):
        return lax.all_to_all(sent, axes, 0, 0, tiled=True)

    def residual(sent, subset, *ready):
        meas, live = masks(subset)
        return pl.pallas_call(
            residual_kernel,
            out_shape=(shape((16, 128)), shape((count, 16, 128), jnp.bfloat16)),
            in_specs=[VM] * (3 + len(ready)),
            out_specs=(VM, VM),
            compiler_params=PARAMS,
        )(exchanged(sent), meas, live, *ready)

    sent = pl.pallas_call(
        first_kernel,
        out_shape=shape((count, 16, 128), jnp.int16),
        in_specs=[SM, VM],
        out_specs=VM,
        scratch_shapes=[F_BUF, F_BUF, L_BUF, ACC_BUF],
        compiler_params=PARAMS,
    )(block_place, volume)
    def footprints(subset, start, *held):
        return pl.pallas_call(
            functools.partial(footprint_kernel, subset, start),
            out_shape=(shape((LOCAL, KALL, VOX), jnp.bfloat16), shape((8, 128))),
            in_specs=[SM] + [ANY] * len(held),
            out_specs=(ANY, VM),
            scratch_shapes=[
                pltpu.VMEM((MADE, KALL, VOX), jnp.bfloat16),
                L_BUF,
                pltpu.SemaphoreType.DMA((MADE,)),
            ],
            input_output_aliases={1: 0} if held else {},
            compiler_params=PARAMS,
            cost_estimate=pl.CostEstimate(
                flops=0, bytes_accessed=LOCAL * KALL * VOX, transcendentals=0
            ),
        )(block_place, *held)

    fa, token = footprints(0, 0)
    _, rounded = residual(sent, 0, token)
    fa, _ = footprints(0, LOCAL // 2, fa)
    estimate, sent = pl.pallas_call(
        middle_kernel,
        out_shape=(shape(volume.shape), shape((count, 16, 128), jnp.int16)),
        in_specs=[SM, VM, VM, ANY],
        out_specs=(VM, VM),
        scratch_shapes=[
            F_RING,
            F_BUF,
            F_BUF,
            L_BUF,
            ACC_BUF,
            RES_BUF,
            pltpu.SemaphoreType.DMA((1, DEPTH)),
        ],
        compiler_params=PARAMS,
    )(block_place, exchanged(rounded), volume, fa)
    fb, token = footprints(1, 0)
    last, rounded = residual(sent, 1, token)
    fb, _ = footprints(1, LOCAL // 2, fb)
    final = pl.pallas_call(
        last_kernel,
        out_shape=shape(volume.shape),
        in_specs=[SM, VM, VM, ANY],
        out_specs=VM,
        scratch_shapes=[F_RING, RES_BUF, pltpu.SemaphoreType.DMA((1, DEPTH))],
        compiler_params=PARAMS,
    )(block_place, exchanged(rounded), estimate, fb)
    last = unpacked_rays(last, odd).T.reshape(1, own, RAYS_TILE * NSL)
    return final, last


def solution(mesh):
    return jax.shard_map(
        shards,
        mesh=mesh,
        in_specs=(
            P(("group", "patch"), None, None),
            P(("group", "patch")),
            P(None, "patch", None),
            P(),
        ),
        out_specs=(P(("group", "patch"), None, None), P("group", "patch", None)),
        check_vma=False,
    )
```

```python
import functools
import math

import jax
import jax.numpy as jnp
import numpy as np
from jax import lax
from jax.experimental import pallas as pl
from jax.experimental.pallas import tpu as pltpu
from jax.sharding import PartitionSpec as P

IMG_BLK = 64
BLK_SIDE = 32
VOX = BLK_SIDE * BLK_SIDE
RAYS_TILE = 48
NTILE = 64
ANG_SUB = 8
SUBSETS = 2
NSL = 8
SPREAD = 1.5
RELAX = 0.9
RAYS = NTILE * RAYS_TILE
WIN = 48
KALL = ANG_SUB * WIN
HALF_IMG = IMG_BLK * BLK_SIDE * 0.5
CHUNKS = 16
LOCAL = 32
DEPTH = 12
MADE = 4
TOGETHER = 4
CODES = 32766.0
LEAD = 23.75


def angle_consts(subset):
    out = []
    for a in range(ANG_SUB):
        theta = np.float32(math.pi * (a * SUBSETS + subset) / (ANG_SUB * SUBSETS))
        out.append((float(np.cos(theta)), float(np.sin(theta))))
    return out


def touched(cos, sin, ray0, chunk):
    v = np.arange(chunk * 128, chunk * 128 + 128)
    along = (v % BLK_SIDE - 15.5) * cos + (v // BLK_SIDE - 15.5) * sin
    low = along.min() + LEAD - 0.5 - SPREAD - 0.01
    high = along.max() + LEAD + 0.5 + SPREAD + 0.01
    return ray0 <= high and ray0 + 7 >= low


def place_of(place_ref, b, cos, sin):
    q = place_ref[b]
    x = ((q & (IMG_BLK - 1)) * BLK_SIDE).astype(jnp.float32) + (BLK_SIDE * 0.5 - HALF_IMG)
    y = ((q >> 6) * BLK_SIDE).astype(jnp.float32) + (BLK_SIDE * 0.5 - HALF_IMG)
    centre = x * cos + y * sin
    first = (centre + (RAYS * 0.5 - LEAD)).astype(jnp.int32)
    beta = centre + (RAYS * 0.5 - 0.5) - first.astype(jnp.float32)
    return first, beta


def fill_offsets(l_ref, subset):
    lane = lax.broadcasted_iota(jnp.int32, (8, 128), 1)
    for a, (cos, sin) in enumerate(angle_consts(subset)):
        for c in range(8):
            v = lane + c * 128
            dx = (v & 31).astype(jnp.float32) - 15.5
            dy = (v >> 5).astype(jnp.float32) - 15.5
            l_ref[a * 8 + c] = (dx * cos + dy * sin) * (1.0 / SPREAD)


def windows(place_ref, b, subset):
    return [place_of(place_ref, b, cos, sin) for cos, sin in angle_consts(subset)]


def make_footprint(f_ref, l_ref, at, subset, part):
    sub = lax.broadcasted_iota(jnp.int32, (8, 128), 0).astype(jnp.float32) * (1.0 / SPREAD)
    zero = jnp.zeros((8, 128), jnp.float32)
    for a, (cos, sin) in enumerate(angle_consts(subset)):
        beta = at[a][1] * (1.0 / SPREAD)
        rays = [sub + (8 * r / SPREAD - beta) for r in range(WIN // 8)]
        for c in (2 * part, 2 * part + 1):
            offs = l_ref[a * 8 + c]
            for t in range(WIN // 16):
                halves = []
                for r in (2 * t, 2 * t + 1):
                    if touched(cos, sin, 8 * r, c):
                        d = offs - rays[r]
                        m = jnp.maximum(1.0 - d * d, 0.0)
                        halves.append(m * m)
                    else:
                        halves.append(None)
                if halves[0] is None and halves[1] is None:
                    continue
                tile = jnp.concatenate([zero if h is None else h for h in halves], axis=0)
                f_ref[pl.ds(a * WIN + 16 * t, 16), pl.ds(c * 128, 128)] = tile.astype(jnp.bfloat16)


def zero_fill(f_ref):
    for r in range(KALL // 16):
        f_ref[pl.ds(16 * r, 16), :] = jnp.zeros((16, VOX), jnp.bfloat16)


def lanes(rows=8):
    return lax.broadcasted_iota(jnp.int32, (rows, 128), 1)


def with_ones(x):
    row = lax.broadcasted_iota(jnp.int32, x.shape, 0)
    return jnp.concatenate([x, jnp.where(row == 0, 1.0, 0.0)], axis=0).astype(jnp.bfloat16)


def project(x, f_ref, cols=slice(None)):
    return lax.dot_general(
        x[:, cols], f_ref[:, cols], (((1,), (1,)), ((), ())), preferred_element_type=jnp.float32
    )


def scatter_windows(acc_ref, contrib, at):
    lane = lanes(16)
    for a in range(ANG_SUB):
        t0, lo = a * WIN // 128, a * WIN % 128
        piece = contrib[:, t0 * 128 : t0 * 128 + 128]
        if lo + WIN > 128:
            after = contrib[:, t0 * 128 + 128 : t0 * 128 + 256]
            piece = jnp.where(lane >= lo, piece, jnp.where(lane < lo + WIN - 128, after, 0.0))
        else:
            piece = jnp.where((lane >= lo) & (lane < lo + WIN), piece, 0.0)
        first = at[a][0]
        r = first & 127
        base = pl.multiple_of(first - r, 128)
        turned = pltpu.roll(piece, (r - lo + 128) & 127, 1)
        acc_ref[a, :, pl.ds(base, 128)] += jnp.where(lane >= r, turned, 0.0)
        acc_ref[a, :, pl.ds(base + 128, 128)] += jnp.where(lane < r, turned, 0.0)


def gather_windows(res_ref, at):
    lane = lanes(8)
    tiles = [jnp.zeros((8, 128), jnp.float32) for _ in range(KALL // 128)]
    for a in range(ANG_SUB):
        t0, lo = a * WIN // 128, a * WIN % 128
        first = at[a][0]
        r = first & 127
        base = pl.multiple_of(first - r, 128)
        here = res_ref[a, :, pl.ds(base, 128)]
        after = res_ref[a, :, pl.ds(base + 128, 128)]
        turned = pltpu.roll(jnp.where(lane >= r, here, after), (lo - r + 128) & 127, 1)
        if lo + WIN > 128:
            tiles[t0] = jnp.where(lane >= lo, turned, tiles[t0])
            tiles[t0 + 1] = jnp.where(lane < lo + WIN - 128, turned, tiles[t0 + 1])
        else:
            tiles[t0] = jnp.where((lane >= lo) & (lane < lo + WIN), turned, tiles[t0])
    return with_ones(jnp.concatenate(tiles, axis=1))


def chunk_at(a, c):
    return (c % 8) * 16 + a * 2 + c // 8


def coded(x, scale):
    root = lax.rsqrt(lax.rsqrt(jnp.maximum(x, 1e-30)))
    return (root * scale + 0.5).astype(jnp.int32)


def decoded(codes, unit):
    part = codes * (1.0 / CODES)
    part = part * part
    return part * part * unit


def write_chunks(out_ref, acc_ref):
    lane4 = lanes(4)
    largest = jnp.zeros((16, 128), jnp.float32)
    for a in range(ANG_SUB):
        for t in range(RAYS // 128):
            largest = jnp.maximum(largest, acc_ref[a, :, pl.ds(t * 128, 128)])
    half_unit = jnp.floor(jnp.max(largest[0:8], axis=(0, 1), keepdims=True) * 0.5) + 1.0
    sum_unit = jnp.floor(jnp.max(largest[8:9], axis=(0, 1), keepdims=True)) + 1.0
    scale, sum_scale = (CODES * lax.rsqrt(jnp.sqrt(u)) for u in (half_unit * 2.0, sum_unit))
    row = lax.broadcasted_iota(jnp.int32, (8, 128), 0)
    mixed = jnp.where(row < 4, scale, sum_scale)
    units = jnp.where(row == 6, half_unit, sum_unit).astype(jnp.int32)
    for a in range(ANG_SUB):
        for m in range(CHUNKS // 2):
            for odd in range(2):
                whole = acc_ref[a, :, pl.ds((3 * m + 2 * odd) * 128, 128)]
                half = acc_ref[a, :, pl.ds((3 * m + 1) * 128, 128)]
                turned = pltpu.roll(half, 64, 1)
                if odd:
                    half, turned = turned, half
                packed = jnp.where(lane4 < 64, half[0:4], turned[4:8])
                sums = jnp.where(lanes(1) < 64, half[8:9], turned[8:9])
                rest = jnp.concatenate([packed, whole[8:9], sums, sums, sums], axis=0)
                rest = jnp.where(row < 6, coded(rest, mixed), units)
                chunk = jnp.concatenate([coded(whole[0:8], scale), rest], axis=0)
                out_ref[chunk_at(a, 2 * m + odd)] = chunk.astype(jnp.int16)


def read_chunks(res_ref, got_ref):
    lane = lanes(8)
    for a in range(ANG_SUB):
        for m in range(CHUNKS // 2):
            even = got_ref[chunk_at(a, 2 * m)].astype(jnp.float32)
            odd = got_ref[chunk_at(a, 2 * m + 1)].astype(jnp.float32)
            res_ref[a, :, pl.ds(3 * m * 128, 128)] = even[0:8]
            res_ref[a, :, pl.ds((3 * m + 2) * 128, 128)] = odd[0:8]
            he = jnp.concatenate([even[8:12], pltpu.roll(even[8:16], 64, 1)[0:4]], axis=0)
            ho = jnp.concatenate([pltpu.roll(odd[8:16], 64, 1)[0:4], odd[8:12]], axis=0)
            res_ref[a, :, pl.ds((3 * m + 1) * 128, 128)] = jnp.where(lane < 64, he, ho)
        res_ref[a, :, pl.ds(RAYS, 128)] = jnp.zeros((8, 128), jnp.float32)


def first_kernel(place_ref, x_ref, out_ref, *refs):
    slots, (l_ref, acc_ref) = refs[:-2], refs[-2:]
    count = len(slots)
    fill_offsets(l_ref, 0)
    for f in slots:
        zero_fill(f)
    acc_ref[...] = jnp.zeros_like(acc_ref)

    def make(f, b):
        at = windows(place_ref, b, 0)
        return lambda part: make_footprint(f, l_ref, at, 0, part)

    def step(b, f, fill):
        x = with_ones(x_ref[b])
        contrib = 0.0
        for part in range(4):
            contrib = contrib + project(x, f, slice(part * 256, part * 256 + 256))
            fill(part)
        scatter_windows(acc_ref, contrib, windows(place_ref, b, 0))

    for part in range(4):
        make(slots[0], 0)(part)

    def some(i, carry):
        for k in range(count):
            b = i * count + k
            step(b, slots[k], make(slots[(k + 1) % count], jnp.minimum(b + 1, LOCAL - 1)))
        return carry

    lax.fori_loop(0, LOCAL // count, some, 0)
    write_chunks(out_ref, acc_ref)


def updated(x, total):
    return jnp.maximum(x + total[0:8] * (RELAX / total[8:9]), 0.0)


def footprint_kernel(subset, start, place_ref, *refs):
    out_ref, token_ref, slots, l_ref, sems = refs[-5:]
    token_ref[...] = jnp.zeros_like(token_ref)
    fill_offsets(l_ref, subset)
    for k in range(MADE):
        zero_fill(slots.at[k])

    def some(i, carry):
        for k in range(MADE):
            b = start + i * MADE + k

            @pl.when(i > 0)
            def _():
                pltpu.make_async_copy(slots.at[k], out_ref.at[b], sems.at[k]).wait()

            at = windows(place_ref, b, subset)
            for part in range(4):
                make_footprint(slots.at[k], l_ref, at, subset, part)
            pltpu.make_async_copy(slots.at[k], out_ref.at[b], sems.at[k]).start()
        return carry

    lax.fori_loop(0, LOCAL // 2 // MADE, some, 0)
    for k in range(MADE):
        b = start + LOCAL // 2 - MADE + k
        pltpu.make_async_copy(slots.at[k], out_ref.at[b], sems.at[k]).wait()


def streamed(sources, slots, sems, before, step):
    many = range(len(sources))

    def copy(n, b):
        k = lax.rem(b, DEPTH)
        return pltpu.make_async_copy(sources[n].at[b], slots[n].at[k], sems.at[n, k])

    for b in range(DEPTH - TOGETHER):
        for n in many:
            copy(n, b).start()
    before()

    def some(i, carry):
        first = i * TOGETHER

        @pl.when(first + DEPTH - TOGETHER < LOCAL)
        def _():
            for k in range(TOGETHER):
                for n in many:
                    copy(n, first + DEPTH - TOGETHER + k).start()

        for k in range(TOGETHER):
            for n in many:
                copy(n, first + k).wait()
        for k in range(TOGETHER):
            b = first + k
            step(b, k, [slots[n].at[lax.rem(b, DEPTH)] for n in many])
        return carry

    lax.fori_loop(0, LOCAL // TOGETHER, some, 0)


def middle_kernel(
    place_ref, got_ref, x_ref, fa, new_ref, out_ref, ring, l_ref, acc_ref, res_ref, sems, *made
):
    count = len(made)

    def make(f, b):
        at = windows(place_ref, b, 1)
        return lambda part: make_footprint(f, l_ref, at, 1, part)

    def before():
        fill_offsets(l_ref, 1)
        for f in made:
            zero_fill(f)
        for part in range(4):
            make(made[0], 0)(part)
        read_chunks(res_ref, got_ref)
        acc_ref[...] = jnp.zeros_like(acc_ref)

    def step(b, k, refs):
        f = made[k % count]
        fill = make(made[(k + 1) % count], jnp.minimum(b + 1, LOCAL - 1))
        res = gather_windows(res_ref, windows(place_ref, b, 0))
        total = jnp.dot(res, refs[0][...], preferred_element_type=jnp.float32)
        x = updated(x_ref[b], total)
        new_ref[b] = x
        x = with_ones(x)
        contrib = 0.0
        for part in range(4):
            contrib = contrib + project(x, f, slice(part * 256, part * 256 + 256))
            fill(part)
        scatter_windows(acc_ref, contrib, windows(place_ref, b, 1))

    streamed((fa,), (ring,), sems, before, step)
    write_chunks(out_ref, acc_ref)


def last_kernel(place_ref, got_ref, x_ref, fb, new_ref, slots, res_ref, sems):
    def before():
        read_chunks(res_ref, got_ref)

    def step(b, k, refs):
        res = gather_windows(res_ref, windows(place_ref, b, 1))
        total = jnp.dot(res, refs[0][...], preferred_element_type=jnp.float32)
        new_ref[b] = updated(x_ref[b], total)

    streamed((fb,), (slots,), sems, before, step)


def residual_kernel(got_ref, meas_ref, live_ref, *refs):
    res_ref, send_ref = refs[-2:]
    count = got_ref.shape[0]

    row = lax.broadcasted_iota(jnp.int32, (16, 128), 0)

    def add(i, totals):
        out = []
        for k, t in enumerate(totals):
            chunk = got_ref[4 * i + k].astype(jnp.int32).astype(jnp.float32)
            unit = jnp.where(row < 12, chunk[14:15] * 2.0, chunk[15:16])
            out.append(t + decoded(chunk, unit))
        return tuple(out)

    zero = jnp.zeros((16, 128), jnp.float32)
    parts = lax.fori_loop(0, count // 4, add, (zero,) * 4, unroll=4)
    total = (parts[0] + parts[1]) + (parts[2] + parts[3])
    sums = jnp.where(row < 8, total[12:13], total[13:14])
    differ = (meas_ref[...] - total / jnp.maximum(sums, 1.0)) * live_ref[...]
    res_ref[...] = differ
    rounded = differ.astype(jnp.bfloat16)

    def put(i, carry):
        send_ref[i] = rounded
        return carry

    lax.fori_loop(0, count, put, 0, unroll=8)


VM = pl.BlockSpec(memory_space=pltpu.VMEM)
ANY = pl.BlockSpec(memory_space=pl.ANY)
SM = pl.BlockSpec(memory_space=pltpu.SMEM)
F_RING = pltpu.VMEM((DEPTH, KALL, VOX), jnp.bfloat16)
F_BUF = pltpu.VMEM((KALL, VOX), jnp.bfloat16)
L_BUF = pltpu.VMEM((ANG_SUB * 8, 8, 128), jnp.float32)
ACC_BUF = pltpu.VMEM((ANG_SUB, 16, RAYS + 128), jnp.float32)
RES_BUF = pltpu.VMEM((ANG_SUB, 8, RAYS + 128), jnp.float32)
PARAMS = pltpu.CompilerParams(vmem_limit_bytes=48 * 1024 * 1024)


def shape(dims, dtype=jnp.float32):
    return jax.ShapeDtypeStruct(dims, dtype)


def packed_rays(x, odd):
    whole = jnp.where(odd, x[:, 64:192], x[:, 0:128])
    half = jnp.where(odd, x[:, 0:64], x[:, 128:192])
    return jnp.concatenate(
        [whole, jnp.concatenate([half[0:4], half[4:8]], axis=1), jnp.zeros((4, 128), x.dtype)], axis=0
    )


def unpacked_rays(chunk, odd):
    whole = chunk[0:8]
    half = jnp.concatenate([chunk[8:12, 0:64], chunk[8:12, 64:128]], axis=0)
    return jnp.where(
        odd, jnp.concatenate([half, whole], axis=1), jnp.concatenate([whole, half], axis=1)
    )


def shards(volume, block_place, measured, live_rays):
    axes = ("group", "patch")
    group = lax.axis_index("group")
    patch = lax.axis_index("patch")
    count = lax.axis_size("group") * lax.axis_size("patch")
    odd = group % 2 == 1
    own = ANG_SUB * NTILE // count

    def masks(subset):
        rows = lax.dynamic_slice_in_dim(measured[subset], group * own, own, 0)
        rows = rows.reshape(own * RAYS_TILE, NSL).T
        live = lax.dynamic_slice_in_dim(
            live_rays[subset], (patch * lax.axis_size("group") + group) * own, own, 0
        )
        live = (jnp.arange(RAYS_TILE, dtype=jnp.int32)[None, :] < live[:, None]).astype(jnp.float32)
        live = jnp.broadcast_to(live.reshape(1, -1), (NSL, own * RAYS_TILE))
        return packed_rays(rows, odd), packed_rays(live, odd)

    def exchanged(sent):
        return lax.all_to_all(sent, axes, 0, 0, tiled=True)

    def residual(sent, subset, *ready):
        meas, live = masks(subset)
        return pl.pallas_call(
            residual_kernel,
            out_shape=(shape((16, 128)), shape((count, 16, 128), jnp.bfloat16)),
            in_specs=[VM] * (3 + len(ready)),
            out_specs=(VM, VM),
            compiler_params=PARAMS,
        )(exchanged(sent), meas, live, *ready)

    sent = pl.pallas_call(
        first_kernel,
        out_shape=shape((count, 16, 128), jnp.int16),
        in_specs=[SM, VM],
        out_specs=VM,
        scratch_shapes=[F_BUF] * 4 + [L_BUF, ACC_BUF],
        compiler_params=PARAMS,
    )(block_place, volume)
    def footprints(subset, start, *held):
        return pl.pallas_call(
            functools.partial(footprint_kernel, subset, start),
            out_shape=(shape((LOCAL, KALL, VOX), jnp.bfloat16), shape((8, 128))),
            in_specs=[SM] + [ANY] * len(held),
            out_specs=(ANY, VM),
            scratch_shapes=[
                pltpu.VMEM((MADE, KALL, VOX), jnp.bfloat16),
                L_BUF,
                pltpu.SemaphoreType.DMA((MADE,)),
            ],
            input_output_aliases={1: 0} if held else {},
            compiler_params=PARAMS,
            cost_estimate=pl.CostEstimate(
                flops=0, bytes_accessed=LOCAL * KALL * VOX, transcendentals=0
            ),
        )(block_place, *held)

    fa, token = footprints(0, 0)
    _, rounded = residual(sent, 0, token)
    fa, _ = footprints(0, LOCAL // 2, fa)
    estimate, sent = pl.pallas_call(
        middle_kernel,
        out_shape=(shape(volume.shape), shape((count, 16, 128), jnp.int16)),
        in_specs=[SM, VM, VM, ANY],
        out_specs=(VM, VM),
        scratch_shapes=[
            F_RING,
            L_BUF,
            ACC_BUF,
            RES_BUF,
            pltpu.SemaphoreType.DMA((1, DEPTH)),
        ]
        + [F_BUF] * 4,
        compiler_params=PARAMS,
    )(block_place, exchanged(rounded), volume, fa)
    fb, token = footprints(1, 0)
    last, rounded = residual(sent, 1, token)
    fb, _ = footprints(1, LOCAL // 2, fb)
    final = pl.pallas_call(
        last_kernel,
        out_shape=shape(volume.shape),
        in_specs=[SM, VM, VM, ANY],
        out_specs=VM,
        scratch_shapes=[F_RING, RES_BUF, pltpu.SemaphoreType.DMA((1, DEPTH))],
        compiler_params=PARAMS,
    )(block_place, exchanged(rounded), estimate, fb)
    last = unpacked_rays(last, odd).T.reshape(1, own, RAYS_TILE * NSL)
    return final, last


def solution(mesh):
    return jax.shard_map(
        shards,
        mesh=mesh,
        in_specs=(
            P(("group", "patch"), None, None),
            P(("group", "patch")),
            P(None, "patch", None),
            P(),
        ),
        out_specs=(P(("group", "patch"), None, None), P("group", "patch", None)),
        check_vma=False,
    )
```

```python
import functools
import math

import jax
import jax.numpy as jnp
import numpy as np
from jax import lax
from jax.experimental import pallas as pl
from jax.experimental.pallas import tpu as pltpu
from jax.sharding import PartitionSpec as P

IMG_BLK = 64
BLK_SIDE = 32
VOX = BLK_SIDE * BLK_SIDE
RAYS_TILE = 48
NTILE = 64
ANG_SUB = 8
SUBSETS = 2
NSL = 8
SPREAD = 1.5
RELAX = 0.9
RAYS = NTILE * RAYS_TILE
WIN = 48
KALL = ANG_SUB * WIN
HALF_IMG = IMG_BLK * BLK_SIDE * 0.5
CHUNKS = 16
LOCAL = 32
DEPTH = 12
FIRST = 12
MADE = 4
TOGETHER = 4
CODES = 32766.0
LEAD = 23.75


def angle_consts(subset):
    out = []
    for a in range(ANG_SUB):
        theta = np.float32(math.pi * (a * SUBSETS + subset) / (ANG_SUB * SUBSETS))
        out.append((float(np.cos(theta)), float(np.sin(theta))))
    return out


def touched(cos, sin, ray0, chunk):
    v = np.arange(chunk * 128, chunk * 128 + 128)
    along = (v % BLK_SIDE - 15.5) * cos + (v // BLK_SIDE - 15.5) * sin
    low = along.min() + LEAD - 0.5 - SPREAD - 0.01
    high = along.max() + LEAD + 0.5 + SPREAD + 0.01
    return ray0 <= high and ray0 + 7 >= low


def place_of(place_ref, b, cos, sin):
    q = place_ref[b]
    x = ((q & (IMG_BLK - 1)) * BLK_SIDE).astype(jnp.float32) + (BLK_SIDE * 0.5 - HALF_IMG)
    y = ((q >> 6) * BLK_SIDE).astype(jnp.float32) + (BLK_SIDE * 0.5 - HALF_IMG)
    centre = x * cos + y * sin
    first = (centre + (RAYS * 0.5 - LEAD)).astype(jnp.int32)
    beta = centre + (RAYS * 0.5 - 0.5) - first.astype(jnp.float32)
    return first, beta


def fill_offsets(l_ref, subset):
    lane = lax.broadcasted_iota(jnp.int32, (8, 128), 1)
    for a, (cos, sin) in enumerate(angle_consts(subset)):
        for c in range(8):
            v = lane + c * 128
            dx = (v & 31).astype(jnp.float32) - 15.5
            dy = (v >> 5).astype(jnp.float32) - 15.5
            l_ref[a * 8 + c] = (dx * cos + dy * sin) * (1.0 / SPREAD)


def windows(place_ref, b, subset):
    return [place_of(place_ref, b, cos, sin) for cos, sin in angle_consts(subset)]


def make_footprint(f_ref, l_ref, at, subset, part):
    sub = lax.broadcasted_iota(jnp.int32, (8, 128), 0).astype(jnp.float32) * (1.0 / SPREAD)
    zero = jnp.zeros((8, 128), jnp.float32)
    for a, (cos, sin) in enumerate(angle_consts(subset)):
        beta = at[a][1] * (1.0 / SPREAD)
        rays = [sub + (8 * r / SPREAD - beta) for r in range(WIN // 8)]
        for c in (2 * part, 2 * part + 1):
            offs = l_ref[a * 8 + c]
            for t in range(WIN // 16):
                halves = []
                for r in (2 * t, 2 * t + 1):
                    if touched(cos, sin, 8 * r, c):
                        d = offs - rays[r]
                        m = jnp.maximum(1.0 - d * d, 0.0)
                        halves.append(m * m)
                    else:
                        halves.append(None)
                if halves[0] is None and halves[1] is None:
                    continue
                tile = jnp.concatenate([zero if h is None else h for h in halves], axis=0)
                f_ref[pl.ds(a * WIN + 16 * t, 16), pl.ds(c * 128, 128)] = tile.astype(jnp.bfloat16)


def zero_fill(f_ref):
    for r in range(KALL // 16):
        f_ref[pl.ds(16 * r, 16), :] = jnp.zeros((16, VOX), jnp.bfloat16)


def lanes(rows=8):
    return lax.broadcasted_iota(jnp.int32, (rows, 128), 1)


def with_ones(x):
    row = lax.broadcasted_iota(jnp.int32, x.shape, 0)
    return jnp.concatenate([x, jnp.where(row == 0, 1.0, 0.0)], axis=0).astype(jnp.bfloat16)


def project(x, f_ref, cols=slice(None)):
    return lax.dot_general(
        x[:, cols], f_ref[:, cols], (((1,), (1,)), ((), ())), preferred_element_type=jnp.float32
    )


def scatter_windows(acc_ref, contrib, at):
    lane = lanes(16)
    for a in range(ANG_SUB):
        t0, lo = a * WIN // 128, a * WIN % 128
        piece = contrib[:, t0 * 128 : t0 * 128 + 128]
        if lo + WIN > 128:
            after = contrib[:, t0 * 128 + 128 : t0 * 128 + 256]
            piece = jnp.where(lane >= lo, piece, jnp.where(lane < lo + WIN - 128, after, 0.0))
        else:
            piece = jnp.where((lane >= lo) & (lane < lo + WIN), piece, 0.0)
        first = at[a][0]
        r = first & 127
        base = pl.multiple_of(first - r, 128)
        turned = pltpu.roll(piece, (r - lo + 128) & 127, 1)
        acc_ref[a, :, pl.ds(base, 128)] += jnp.where(lane >= r, turned, 0.0)
        acc_ref[a, :, pl.ds(base + 128, 128)] += jnp.where(lane < r, turned, 0.0)


def gather_windows(res_ref, at):
    lane = lanes(8)
    tiles = [jnp.zeros((8, 128), jnp.float32) for _ in range(KALL // 128)]
    for a in range(ANG_SUB):
        t0, lo = a * WIN // 128, a * WIN % 128
        first = at[a][0]
        r = first & 127
        base = pl.multiple_of(first - r, 128)
        here = res_ref[a, :, pl.ds(base, 128)]
        after = res_ref[a, :, pl.ds(base + 128, 128)]
        turned = pltpu.roll(jnp.where(lane >= r, here, after), (lo - r + 128) & 127, 1)
        if lo + WIN > 128:
            tiles[t0] = jnp.where(lane >= lo, turned, tiles[t0])
            tiles[t0 + 1] = jnp.where(lane < lo + WIN - 128, turned, tiles[t0 + 1])
        else:
            tiles[t0] = jnp.where((lane >= lo) & (lane < lo + WIN), turned, tiles[t0])
    return with_ones(jnp.concatenate(tiles, axis=1))


def chunk_at(a, c):
    return (c % 8) * 16 + a * 2 + c // 8


def coded(x, scale):
    root = lax.rsqrt(lax.rsqrt(jnp.maximum(x, 1e-30)))
    return (root * scale + 0.5).astype(jnp.int32)


def decoded(codes, unit):
    part = codes * (1.0 / CODES)
    part = part * part
    return part * part * unit


def write_chunks(out_ref, acc_ref):
    lane4 = lanes(4)
    largest = jnp.zeros((16, 128), jnp.float32)
    for a in range(ANG_SUB):
        for t in range(RAYS // 128):
            largest = jnp.maximum(largest, acc_ref[a, :, pl.ds(t * 128, 128)])
    half_unit = jnp.floor(jnp.max(largest[0:8], axis=(0, 1), keepdims=True) * 0.5) + 1.0
    sum_unit = jnp.floor(jnp.max(largest[8:9], axis=(0, 1), keepdims=True)) + 1.0
    scale, sum_scale = (CODES * lax.rsqrt(jnp.sqrt(u)) for u in (half_unit * 2.0, sum_unit))
    row = lax.broadcasted_iota(jnp.int32, (8, 128), 0)
    mixed = jnp.where(row < 4, scale, sum_scale)
    units = jnp.where(row == 6, half_unit, sum_unit).astype(jnp.int32)
    for a in range(ANG_SUB):
        for m in range(CHUNKS // 2):
            for odd in range(2):
                whole = acc_ref[a, :, pl.ds((3 * m + 2 * odd) * 128, 128)]
                half = acc_ref[a, :, pl.ds((3 * m + 1) * 128, 128)]
                turned = pltpu.roll(half, 64, 1)
                if odd:
                    half, turned = turned, half
                packed = jnp.where(lane4 < 64, half[0:4], turned[4:8])
                sums = jnp.where(lanes(1) < 64, half[8:9], turned[8:9])
                rest = jnp.concatenate([packed, whole[8:9], sums, sums, sums], axis=0)
                rest = jnp.where(row < 6, coded(rest, mixed), units)
                chunk = jnp.concatenate([coded(whole[0:8], scale), rest], axis=0)
                out_ref[chunk_at(a, 2 * m + odd)] = chunk.astype(jnp.int16)


def read_chunks(res_ref, got_ref):
    lane = lanes(8)
    for a in range(ANG_SUB):
        for m in range(CHUNKS // 2):
            even = got_ref[chunk_at(a, 2 * m)].astype(jnp.float32)
            odd = got_ref[chunk_at(a, 2 * m + 1)].astype(jnp.float32)
            res_ref[a, :, pl.ds(3 * m * 128, 128)] = even[0:8]
            res_ref[a, :, pl.ds((3 * m + 2) * 128, 128)] = odd[0:8]
            he = jnp.concatenate([even[8:12], pltpu.roll(even[8:16], 64, 1)[0:4]], axis=0)
            ho = jnp.concatenate([pltpu.roll(odd[8:16], 64, 1)[0:4], odd[8:12]], axis=0)
            res_ref[a, :, pl.ds((3 * m + 1) * 128, 128)] = jnp.where(lane < 64, he, ho)
        res_ref[a, :, pl.ds(RAYS, 128)] = jnp.zeros((8, 128), jnp.float32)


def first_kernel(place_ref, x_ref, out_ref, *refs):
    slots, (l_ref, acc_ref) = refs[:-2], refs[-2:]
    count = len(slots)
    fill_offsets(l_ref, 0)
    for f in slots:
        zero_fill(f)
    acc_ref[...] = jnp.zeros_like(acc_ref)

    def make(f, b):
        at = windows(place_ref, b, 0)
        return lambda part: make_footprint(f, l_ref, at, 0, part)

    def step(b, f, fill):
        x = with_ones(x_ref[b])
        contrib = 0.0
        for part in range(4):
            contrib = contrib + project(x, f, slice(part * 256, part * 256 + 256))
            fill(part)
        scatter_windows(acc_ref, contrib, windows(place_ref, b, 0))

    for part in range(4):
        make(slots[0], 0)(part)

    def some(i, carry):
        for k in range(count):
            b = i * count + k
            step(b, slots[k], make(slots[(k + 1) % count], jnp.minimum(b + 1, LOCAL - 1)))
        return carry

    lax.fori_loop(0, LOCAL // count, some, 0)
    write_chunks(out_ref, acc_ref)


def updated(x, total):
    return jnp.maximum(x + total[0:8] * (RELAX / total[8:9]), 0.0)


def footprint_kernel(subset, start, stop, place_ref, *refs):
    out_ref, token_ref, slots, l_ref, sems = refs[-5:]
    token_ref[...] = jnp.zeros_like(token_ref)
    fill_offsets(l_ref, subset)
    for k in range(MADE):
        zero_fill(slots.at[k])

    def some(i, carry):
        for k in range(MADE):
            b = start + i * MADE + k

            @pl.when(i > 0)
            def _():
                pltpu.make_async_copy(slots.at[k], out_ref.at[b], sems.at[k]).wait()

            at = windows(place_ref, b, subset)
            for part in range(4):
                make_footprint(slots.at[k], l_ref, at, subset, part)
            pltpu.make_async_copy(slots.at[k], out_ref.at[b], sems.at[k]).start()
        return carry

    lax.fori_loop(0, (stop - start) // MADE, some, 0)
    for k in range(MADE):
        b = stop - MADE + k
        pltpu.make_async_copy(slots.at[k], out_ref.at[b], sems.at[k]).wait()


def streamed(sources, slots, sems, before, step):
    many = range(len(sources))

    def copy(n, b):
        k = lax.rem(b, DEPTH)
        return pltpu.make_async_copy(sources[n].at[b], slots[n].at[k], sems.at[n, k])

    for b in range(DEPTH - TOGETHER):
        for n in many:
            copy(n, b).start()
    before()

    def some(i, carry):
        first = i * TOGETHER

        @pl.when(first + DEPTH - TOGETHER < LOCAL)
        def _():
            for k in range(TOGETHER):
                for n in many:
                    copy(n, first + DEPTH - TOGETHER + k).start()

        for k in range(TOGETHER):
            for n in many:
                copy(n, first + k).wait()
        for k in range(TOGETHER):
            b = first + k
            step(b, k, [slots[n].at[lax.rem(b, DEPTH)] for n in many])
        return carry

    lax.fori_loop(0, LOCAL // TOGETHER, some, 0)


def middle_kernel(
    place_ref, got_ref, x_ref, fa, new_ref, out_ref, ring, l_ref, acc_ref, res_ref, sems, *made
):
    count = len(made)

    def make(f, b):
        at = windows(place_ref, b, 1)
        return lambda part: make_footprint(f, l_ref, at, 1, part)

    def before():
        fill_offsets(l_ref, 1)
        for f in made:
            zero_fill(f)
        for part in range(4):
            make(made[0], 0)(part)
        read_chunks(res_ref, got_ref)
        acc_ref[...] = jnp.zeros_like(acc_ref)

    def step(b, k, refs):
        f = made[k % count]
        fill = make(made[(k + 1) % count], jnp.minimum(b + 1, LOCAL - 1))
        res = gather_windows(res_ref, windows(place_ref, b, 0))
        total = jnp.dot(res, refs[0][...], preferred_element_type=jnp.float32)
        x = updated(x_ref[b], total)
        new_ref[b] = x
        x = with_ones(x)
        contrib = 0.0
        for part in range(4):
            contrib = contrib + project(x, f, slice(part * 256, part * 256 + 256))
            fill(part)
        scatter_windows(acc_ref, contrib, windows(place_ref, b, 1))

    streamed((fa,), (ring,), sems, before, step)
    write_chunks(out_ref, acc_ref)


def last_kernel(place_ref, got_ref, x_ref, fb, new_ref, slots, res_ref, sems):
    def before():
        read_chunks(res_ref, got_ref)

    def step(b, k, refs):
        res = gather_windows(res_ref, windows(place_ref, b, 1))
        total = jnp.dot(res, refs[0][...], preferred_element_type=jnp.float32)
        new_ref[b] = updated(x_ref[b], total)

    streamed((fb,), (slots,), sems, before, step)


def residual_kernel(got_ref, meas_ref, live_ref, *refs):
    res_ref, send_ref = refs[-2:]
    count = got_ref.shape[0]

    row = lax.broadcasted_iota(jnp.int32, (16, 128), 0)

    def add(i, totals):
        out = []
        for k, t in enumerate(totals):
            chunk = got_ref[4 * i + k].astype(jnp.int32).astype(jnp.float32)
            unit = jnp.where(row < 12, chunk[14:15] * 2.0, chunk[15:16])
            out.append(t + decoded(chunk, unit))
        return tuple(out)

    zero = jnp.zeros((16, 128), jnp.float32)
    parts = lax.fori_loop(0, count // 4, add, (zero,) * 4, unroll=4)
    total = (parts[0] + parts[1]) + (parts[2] + parts[3])
    sums = jnp.where(row < 8, total[12:13], total[13:14])
    differ = (meas_ref[...] - total / jnp.maximum(sums, 1.0)) * live_ref[...]
    res_ref[...] = differ
    rounded = differ.astype(jnp.bfloat16)

    def put(i, carry):
        send_ref[i] = rounded
        return carry

    lax.fori_loop(0, count, put, 0, unroll=8)


VM = pl.BlockSpec(memory_space=pltpu.VMEM)
ANY = pl.BlockSpec(memory_space=pl.ANY)
SM = pl.BlockSpec(memory_space=pltpu.SMEM)
F_RING = pltpu.VMEM((DEPTH, KALL, VOX), jnp.bfloat16)
F_BUF = pltpu.VMEM((KALL, VOX), jnp.bfloat16)
L_BUF = pltpu.VMEM((ANG_SUB * 8, 8, 128), jnp.float32)
ACC_BUF = pltpu.VMEM((ANG_SUB, 16, RAYS + 128), jnp.float32)
RES_BUF = pltpu.VMEM((ANG_SUB, 8, RAYS + 128), jnp.float32)
PARAMS = pltpu.CompilerParams(vmem_limit_bytes=48 * 1024 * 1024)


def shape(dims, dtype=jnp.float32):
    return jax.ShapeDtypeStruct(dims, dtype)


def packed_rays(x, odd):
    whole = jnp.where(odd, x[:, 64:192], x[:, 0:128])
    half = jnp.where(odd, x[:, 0:64], x[:, 128:192])
    return jnp.concatenate(
        [whole, jnp.concatenate([half[0:4], half[4:8]], axis=1), jnp.zeros((4, 128), x.dtype)], axis=0
    )


def unpacked_rays(chunk, odd):
    whole = chunk[0:8]
    half = jnp.concatenate([chunk[8:12, 0:64], chunk[8:12, 64:128]], axis=0)
    return jnp.where(
        odd, jnp.concatenate([half, whole], axis=1), jnp.concatenate([whole, half], axis=1)
    )


def shards(volume, block_place, measured, live_rays):
    axes = ("group", "patch")
    group = lax.axis_index("group")
    patch = lax.axis_index("patch")
    count = lax.axis_size("group") * lax.axis_size("patch")
    odd = group % 2 == 1
    own = ANG_SUB * NTILE // count

    def masks(subset):
        rows = lax.dynamic_slice(
            measured, (subset, group * own, 0), (1, own, RAYS_TILE * NSL)
        )
        rows = rows.reshape(own * RAYS_TILE, NSL).T
        first = (patch * lax.axis_size("group") + group) * own
        live = lax.dynamic_slice(live_rays, (subset, first), (1, own))[0]
        live = (jnp.arange(RAYS_TILE, dtype=jnp.int32)[None, :] < live[:, None]).astype(jnp.float32)
        live = jnp.broadcast_to(live.reshape(1, -1), (NSL, own * RAYS_TILE))
        return packed_rays(rows, odd), packed_rays(live, odd)

    def exchanged(sent):
        return lax.all_to_all(sent, axes, 0, 0, tiled=True)

    def residual(sent, subset, *ready):
        meas, live = masks(subset)
        return pl.pallas_call(
            residual_kernel,
            out_shape=(shape((16, 128)), shape((count, 16, 128), jnp.bfloat16)),
            in_specs=[VM] * (3 + len(ready)),
            out_specs=(VM, VM),
            compiler_params=PARAMS,
        )(exchanged(sent), meas, live, *ready)

    sent = pl.pallas_call(
        first_kernel,
        out_shape=shape((count, 16, 128), jnp.int16),
        in_specs=[SM, VM],
        out_specs=VM,
        scratch_shapes=[F_BUF] * 4 + [L_BUF, ACC_BUF],
        compiler_params=PARAMS,
    )(block_place, volume)
    def footprints(subset, start, stop, *held):
        return pl.pallas_call(
            functools.partial(footprint_kernel, subset, start, stop),
            out_shape=(shape((LOCAL, KALL, VOX), jnp.bfloat16), shape((8, 128))),
            in_specs=[SM] + [ANY] * len(held),
            out_specs=(ANY, VM),
            scratch_shapes=[
                pltpu.VMEM((MADE, KALL, VOX), jnp.bfloat16),
                L_BUF,
                pltpu.SemaphoreType.DMA((MADE,)),
            ],
            input_output_aliases={1: 0} if held else {},
            compiler_params=PARAMS,
            cost_estimate=pl.CostEstimate(
                flops=0, bytes_accessed=(stop - start) * KALL * VOX * 2, transcendentals=0
            ),
        )(block_place, *held)

    fa, token = footprints(0, 0, FIRST)
    _, rounded = residual(sent, 0, token)
    fa, _ = footprints(0, FIRST, LOCAL, fa)
    estimate, sent = pl.pallas_call(
        middle_kernel,
        out_shape=(shape(volume.shape), shape((count, 16, 128), jnp.int16)),
        in_specs=[SM, VM, VM, ANY],
        out_specs=(VM, VM),
        scratch_shapes=[
            F_RING,
            L_BUF,
            ACC_BUF,
            RES_BUF,
            pltpu.SemaphoreType.DMA((1, DEPTH)),
        ]
        + [F_BUF] * 4,
        compiler_params=PARAMS,
    )(block_place, exchanged(rounded), volume, fa)
    fb, token = footprints(1, 0, LOCAL // 2)
    last, rounded = residual(sent, 1, token)
    fb, _ = footprints(1, LOCAL // 2, LOCAL, fb)
    final = pl.pallas_call(
        last_kernel,
        out_shape=shape(volume.shape),
        in_specs=[SM, VM, VM, ANY],
        out_specs=VM,
        scratch_shapes=[F_RING, RES_BUF, pltpu.SemaphoreType.DMA((1, DEPTH))],
        compiler_params=PARAMS,
    )(block_place, exchanged(rounded), estimate, fb)
    last = unpacked_rays(last, odd).T.reshape(1, own, RAYS_TILE * NSL)
    return final, last


def solution(mesh):
    return jax.shard_map(
        shards,
        mesh=mesh,
        in_specs=(
            P(("group", "patch"), None, None),
            P(("group", "patch")),
            P(None, "patch", None),
            P(),
        ),
        out_specs=(P(("group", "patch"), None, None), P("group", "patch", None)),
        check_vma=False,
    )
```

```python
import functools
import math

import jax
import jax.numpy as jnp
import numpy as np
from jax import lax
from jax.experimental import pallas as pl
from jax.experimental.pallas import tpu as pltpu
from jax.sharding import PartitionSpec as P

IMG_BLK = 64
BLK_SIDE = 32
VOX = BLK_SIDE * BLK_SIDE
RAYS_TILE = 48
NTILE = 64
ANG_SUB = 8
SUBSETS = 2
NSL = 8
SPREAD = 1.5
RELAX = 0.9
RAYS = NTILE * RAYS_TILE
WIN = 48
KALL = ANG_SUB * WIN
HALF_IMG = IMG_BLK * BLK_SIDE * 0.5
CHUNKS = 16
LOCAL = 32
DEPTH = 12
FIRST = 12
MADE = 4
TOGETHER = 4
CODES = 32766.0
LEAD = 23.75


def angle_consts(subset):
    out = []
    for a in range(ANG_SUB):
        theta = np.float32(math.pi * (a * SUBSETS + subset) / (ANG_SUB * SUBSETS))
        out.append((float(np.cos(theta)), float(np.sin(theta))))
    return out


def touched(cos, sin, ray0, chunk):
    v = np.arange(chunk * 128, chunk * 128 + 128)
    along = (v % BLK_SIDE - 15.5) * cos + (v // BLK_SIDE - 15.5) * sin
    low = along.min() + LEAD - 0.5 - SPREAD - 0.01
    high = along.max() + LEAD + 0.5 + SPREAD + 0.01
    return ray0 <= high and ray0 + 7 >= low


def place_of(place_ref, b, cos, sin):
    q = place_ref[b]
    x = ((q & (IMG_BLK - 1)) * BLK_SIDE).astype(jnp.float32) + (BLK_SIDE * 0.5 - HALF_IMG)
    y = ((q >> 6) * BLK_SIDE).astype(jnp.float32) + (BLK_SIDE * 0.5 - HALF_IMG)
    centre = x * cos + y * sin
    first = (centre + (RAYS * 0.5 - LEAD)).astype(jnp.int32)
    beta = centre + (RAYS * 0.5 - 0.5) - first.astype(jnp.float32)
    return first, beta


def fill_offsets(l_ref, subset):
    lane = lax.broadcasted_iota(jnp.int32, (8, 128), 1)
    for a, (cos, sin) in enumerate(angle_consts(subset)):
        for c in range(8):
            v = lane + c * 128
            dx = (v & 31).astype(jnp.float32) - 15.5
            dy = (v >> 5).astype(jnp.float32) - 15.5
            l_ref[a * 8 + c] = (dx * cos + dy * sin) * (1.0 / SPREAD)


def windows(place_ref, b, subset):
    return [place_of(place_ref, b, cos, sin) for cos, sin in angle_consts(subset)]


def make_footprint(f_ref, l_ref, at, subset, part):
    sub = lax.broadcasted_iota(jnp.int32, (8, 128), 0).astype(jnp.float32) * (1.0 / SPREAD)
    zero = jnp.zeros((8, 128), jnp.float32)
    for a, (cos, sin) in enumerate(angle_consts(subset)):
        beta = at[a][1] * (1.0 / SPREAD)
        rays = [sub + (8 * r / SPREAD - beta) for r in range(WIN // 8)]
        for c in (2 * part, 2 * part + 1):
            offs = l_ref[a * 8 + c]
            for t in range(WIN // 16):
                halves = []
                for r in (2 * t, 2 * t + 1):
                    if touched(cos, sin, 8 * r, c):
                        d = offs - rays[r]
                        m = jnp.maximum(1.0 - d * d, 0.0)
                        halves.append(m * m)
                    else:
                        halves.append(None)
                if halves[0] is None and halves[1] is None:
                    continue
                tile = jnp.concatenate([zero if h is None else h for h in halves], axis=0)
                f_ref[pl.ds(a * WIN + 16 * t, 16), pl.ds(c * 128, 128)] = tile.astype(jnp.bfloat16)


def zero_fill(f_ref):
    for r in range(KALL // 16):
        f_ref[pl.ds(16 * r, 16), :] = jnp.zeros((16, VOX), jnp.bfloat16)


def lanes(rows=8):
    return lax.broadcasted_iota(jnp.int32, (rows, 128), 1)


def with_ones(x):
    row = lax.broadcasted_iota(jnp.int32, x.shape, 0)
    return jnp.concatenate([x, jnp.where(row == 0, 1.0, 0.0)], axis=0).astype(jnp.bfloat16)


def project(x, f_ref, cols=slice(None)):
    return lax.dot_general(
        x[:, cols], f_ref[:, cols], (((1,), (1,)), ((), ())), preferred_element_type=jnp.float32
    )


def scatter_windows(acc_ref, contrib, at):
    lane = lanes(16)
    for a in range(ANG_SUB):
        t0, lo = a * WIN // 128, a * WIN % 128
        piece = contrib[:, t0 * 128 : t0 * 128 + 128]
        if lo + WIN > 128:
            after = contrib[:, t0 * 128 + 128 : t0 * 128 + 256]
            piece = jnp.where(lane >= lo, piece, jnp.where(lane < lo + WIN - 128, after, 0.0))
        else:
            piece = jnp.where((lane >= lo) & (lane < lo + WIN), piece, 0.0)
        first = at[a][0]
        r = first & 127
        base = pl.multiple_of(first - r, 128)
        turned = pltpu.roll(piece, (r - lo + 128) & 127, 1)
        acc_ref[a, :, pl.ds(base, 128)] += jnp.where(lane >= r, turned, 0.0)
        acc_ref[a, :, pl.ds(base + 128, 128)] += jnp.where(lane < r, turned, 0.0)


def gather_windows(res_ref, at):
    lane = lanes(8)
    tiles = [jnp.zeros((8, 128), jnp.float32) for _ in range(KALL // 128)]
    for a in range(ANG_SUB):
        t0, lo = a * WIN // 128, a * WIN % 128
        first = at[a][0]
        r = first & 127
        base = pl.multiple_of(first - r, 128)
        here = res_ref[a, :, pl.ds(base, 128)]
        after = res_ref[a, :, pl.ds(base + 128, 128)]
        turned = pltpu.roll(jnp.where(lane >= r, here, after), (lo - r + 128) & 127, 1)
        if lo + WIN > 128:
            tiles[t0] = jnp.where(lane >= lo, turned, tiles[t0])
            tiles[t0 + 1] = jnp.where(lane < lo + WIN - 128, turned, tiles[t0 + 1])
        else:
            tiles[t0] = jnp.where((lane >= lo) & (lane < lo + WIN), turned, tiles[t0])
    return with_ones(jnp.concatenate(tiles, axis=1))


def chunk_at(a, c):
    return (c % 8) * 16 + a * 2 + c // 8


def coded(x, scale):
    root = lax.rsqrt(lax.rsqrt(jnp.maximum(x, 1e-30)))
    return (root * scale + 0.5).astype(jnp.int32)


def decoded(codes, unit):
    part = codes * (1.0 / CODES)
    part = part * part
    return part * part * unit


def write_chunks(out_ref, acc_ref):
    lane4 = lanes(4)
    largest = jnp.zeros((16, 128), jnp.float32)
    for a in range(ANG_SUB):
        for t in range(RAYS // 128):
            largest = jnp.maximum(largest, acc_ref[a, :, pl.ds(t * 128, 128)])
    half_unit = jnp.floor(jnp.max(largest[0:8], axis=(0, 1), keepdims=True) * 0.5) + 1.0
    sum_unit = jnp.floor(jnp.max(largest[8:9], axis=(0, 1), keepdims=True)) + 1.0
    scale, sum_scale = (CODES * lax.rsqrt(jnp.sqrt(u)) for u in (half_unit * 2.0, sum_unit))
    row = lax.broadcasted_iota(jnp.int32, (8, 128), 0)
    mixed = jnp.where(row < 4, scale, sum_scale)
    units = jnp.where(row == 6, half_unit, sum_unit).astype(jnp.int32)
    for a in range(ANG_SUB):
        for m in range(CHUNKS // 2):
            for odd in range(2):
                whole = acc_ref[a, :, pl.ds((3 * m + 2 * odd) * 128, 128)]
                half = acc_ref[a, :, pl.ds((3 * m + 1) * 128, 128)]
                turned = pltpu.roll(half, 64, 1)
                if odd:
                    half, turned = turned, half
                packed = jnp.where(lane4 < 64, half[0:4], turned[4:8])
                sums = jnp.where(lanes(1) < 64, half[8:9], turned[8:9])
                rest = jnp.concatenate([packed, whole[8:9], sums, sums, sums], axis=0)
                rest = jnp.where(row < 6, coded(rest, mixed), units)
                chunk = jnp.concatenate([coded(whole[0:8], scale), rest], axis=0)
                out_ref[chunk_at(a, 2 * m + odd)] = chunk.astype(jnp.int16)


def read_chunks(res_ref, got_ref):
    lane = lanes(8)
    for a in range(ANG_SUB):
        for m in range(CHUNKS // 2):
            even = got_ref[chunk_at(a, 2 * m)].astype(jnp.float32)
            odd = got_ref[chunk_at(a, 2 * m + 1)].astype(jnp.float32)
            res_ref[a, :, pl.ds(3 * m * 128, 128)] = even[0:8]
            res_ref[a, :, pl.ds((3 * m + 2) * 128, 128)] = odd[0:8]
            he = jnp.concatenate([even[8:12], pltpu.roll(even[8:16], 64, 1)[0:4]], axis=0)
            ho = jnp.concatenate([pltpu.roll(odd[8:16], 64, 1)[0:4], odd[8:12]], axis=0)
            res_ref[a, :, pl.ds((3 * m + 1) * 128, 128)] = jnp.where(lane < 64, he, ho)
        res_ref[a, :, pl.ds(RAYS, 128)] = jnp.zeros((8, 128), jnp.float32)


def first_kernel(place_ref, x_ref, out_ref, *refs):
    slots, (l_ref, acc_ref) = refs[:-2], refs[-2:]
    count = len(slots)
    fill_offsets(l_ref, 0)
    for f in slots:
        zero_fill(f)
    acc_ref[...] = jnp.zeros_like(acc_ref)

    def make(f, b):
        at = windows(place_ref, b, 0)
        return lambda part: make_footprint(f, l_ref, at, 0, part)

    def step(b, f, fill):
        x = with_ones(x_ref[b])
        contrib = 0.0
        for part in range(4):
            contrib = contrib + project(x, f, slice(part * 256, part * 256 + 256))
            fill(part)
        scatter_windows(acc_ref, contrib, windows(place_ref, b, 0))

    for part in range(4):
        make(slots[0], 0)(part)

    def some(i, carry):
        for k in range(count):
            b = i * count + k
            step(b, slots[k], make(slots[(k + 1) % count], jnp.minimum(b + 1, LOCAL - 1)))
        return carry

    lax.fori_loop(0, LOCAL // count, some, 0)
    write_chunks(out_ref, acc_ref)


def updated(x, total):
    return jnp.maximum(x + total[0:8] * (RELAX / total[8:9]), 0.0)


def footprint_kernel(subset, start, stop, place_ref, *refs):
    out_ref, token_ref, slots, l_ref, sems = refs[-5:]
    token_ref[...] = jnp.zeros_like(token_ref)
    fill_offsets(l_ref, subset)
    for k in range(MADE):
        zero_fill(slots.at[k])

    def some(i, carry):
        for k in range(MADE):
            b = start + i * MADE + k

            @pl.when(i > 0)
            def _():
                pltpu.make_async_copy(slots.at[k], out_ref.at[b], sems.at[k]).wait()

            at = windows(place_ref, b, subset)
            for part in range(4):
                make_footprint(slots.at[k], l_ref, at, subset, part)
            pltpu.make_async_copy(slots.at[k], out_ref.at[b], sems.at[k]).start()
        return carry

    lax.fori_loop(0, (stop - start) // MADE, some, 0)
    for k in range(MADE):
        b = stop - MADE + k
        pltpu.make_async_copy(slots.at[k], out_ref.at[b], sems.at[k]).wait()


def streamed(sources, slots, sems, before, step):
    many = range(len(sources))

    def copy(n, b):
        k = lax.rem(b, DEPTH)
        return pltpu.make_async_copy(sources[n].at[b], slots[n].at[k], sems.at[n, k])

    for b in range(DEPTH - TOGETHER):
        for n in many:
            copy(n, b).start()
    before()

    def some(i, carry):
        first = i * TOGETHER

        @pl.when(first + DEPTH - TOGETHER < LOCAL)
        def _():
            for k in range(TOGETHER):
                for n in many:
                    copy(n, first + DEPTH - TOGETHER + k).start()

        for k in range(TOGETHER):
            for n in many:
                copy(n, first + k).wait()
        for k in range(TOGETHER):
            b = first + k
            step(b, k, [slots[n].at[lax.rem(b, DEPTH)] for n in many])
        return carry

    lax.fori_loop(0, LOCAL // TOGETHER, some, 0)


def middle_kernel(
    place_ref, got_ref, x_ref, fa, new_ref, out_ref, ring, l_ref, acc_ref, res_ref, sems, *made
):
    count = len(made)

    def make(f, b):
        at = windows(place_ref, b, 1)
        return lambda part: make_footprint(f, l_ref, at, 1, part)

    def before():
        fill_offsets(l_ref, 1)
        for f in made:
            zero_fill(f)
        for part in range(4):
            make(made[0], 0)(part)
        read_chunks(res_ref, got_ref)
        acc_ref[...] = jnp.zeros_like(acc_ref)

    def step(b, k, refs):
        f = made[k % count]
        fill = make(made[(k + 1) % count], jnp.minimum(b + 1, LOCAL - 1))
        res = gather_windows(res_ref, windows(place_ref, b, 0))
        total = jnp.dot(res, refs[0][...], preferred_element_type=jnp.float32)
        x = updated(x_ref[b], total)
        new_ref[b] = x
        x = with_ones(x)
        contrib = 0.0
        for part in range(4):
            contrib = contrib + project(x, f, slice(part * 256, part * 256 + 256))
            fill(part)
        scatter_windows(acc_ref, contrib, windows(place_ref, b, 1))

    streamed((fa,), (ring,), sems, before, step)
    write_chunks(out_ref, acc_ref)


def last_kernel(place_ref, got_ref, x_ref, fb, new_ref, slots, res_ref, sems):
    def before():
        read_chunks(res_ref, got_ref)

    def step(b, k, refs):
        res = gather_windows(res_ref, windows(place_ref, b, 1))
        total = jnp.dot(res, refs[0][...], preferred_element_type=jnp.float32)
        new_ref[b] = updated(x_ref[b], total)

    streamed((fb,), (slots,), sems, before, step)


def residual_kernel(got_ref, meas_ref, live_ref, *refs):
    res_ref, send_ref = refs[-2:]
    count = got_ref.shape[0]

    row = lax.broadcasted_iota(jnp.int32, (16, 128), 0)

    def add(i, totals):
        out = []
        for k, t in enumerate(totals):
            chunk = got_ref[4 * i + k].astype(jnp.int32).astype(jnp.float32)
            unit = jnp.where(row < 12, chunk[14:15] * 2.0, chunk[15:16])
            out.append(t + decoded(chunk, unit))
        return tuple(out)

    zero = jnp.zeros((16, 128), jnp.float32)
    parts = lax.fori_loop(0, count // 4, add, (zero,) * 4, unroll=8)
    total = (parts[0] + parts[1]) + (parts[2] + parts[3])
    sums = jnp.where(row < 8, total[12:13], total[13:14])
    differ = (meas_ref[...] - total / jnp.maximum(sums, 1.0)) * live_ref[...]
    res_ref[...] = differ
    rounded = differ.astype(jnp.bfloat16)

    def put(i, carry):
        send_ref[i] = rounded
        return carry

    lax.fori_loop(0, count, put, 0, unroll=8)


VM = pl.BlockSpec(memory_space=pltpu.VMEM)
ANY = pl.BlockSpec(memory_space=pl.ANY)
SM = pl.BlockSpec(memory_space=pltpu.SMEM)
F_RING = pltpu.VMEM((DEPTH, KALL, VOX), jnp.bfloat16)
F_BUF = pltpu.VMEM((KALL, VOX), jnp.bfloat16)
L_BUF = pltpu.VMEM((ANG_SUB * 8, 8, 128), jnp.float32)
ACC_BUF = pltpu.VMEM((ANG_SUB, 16, RAYS + 128), jnp.float32)
RES_BUF = pltpu.VMEM((ANG_SUB, 8, RAYS + 128), jnp.float32)
PARAMS = pltpu.CompilerParams(vmem_limit_bytes=48 * 1024 * 1024)


def shape(dims, dtype=jnp.float32):
    return jax.ShapeDtypeStruct(dims, dtype)


def packed_rays(x, odd):
    whole = jnp.where(odd, x[:, 64:192], x[:, 0:128])
    half = jnp.where(odd, x[:, 0:64], x[:, 128:192])
    return jnp.concatenate(
        [whole, jnp.concatenate([half[0:4], half[4:8]], axis=1), jnp.zeros((4, 128), x.dtype)], axis=0
    )


def unpacked_rays(chunk, odd):
    whole = chunk[0:8]
    half = jnp.concatenate([chunk[8:12, 0:64], chunk[8:12, 64:128]], axis=0)
    return jnp.where(
        odd, jnp.concatenate([half, whole], axis=1), jnp.concatenate([whole, half], axis=1)
    )


def shards(volume, block_place, measured, live_rays):
    axes = ("group", "patch")
    group = lax.axis_index("group")
    patch = lax.axis_index("patch")
    count = lax.axis_size("group") * lax.axis_size("patch")
    odd = group % 2 == 1
    own = ANG_SUB * NTILE // count

    def masks(subset):
        rows = lax.dynamic_slice(
            measured, (subset, group * own, 0), (1, own, RAYS_TILE * NSL)
        )
        rows = rows.reshape(own * RAYS_TILE, NSL).T
        first = (patch * lax.axis_size("group") + group) * own
        live = lax.dynamic_slice(live_rays, (subset, first), (1, own))[0]
        live = (jnp.arange(RAYS_TILE, dtype=jnp.int32)[None, :] < live[:, None]).astype(jnp.float32)
        live = jnp.broadcast_to(live.reshape(1, -1), (NSL, own * RAYS_TILE))
        return packed_rays(rows, odd), packed_rays(live, odd)

    def exchanged(sent):
        return lax.all_to_all(sent, axes, 0, 0, tiled=True)

    def residual(sent, subset, *ready):
        meas, live = masks(subset)
        return pl.pallas_call(
            residual_kernel,
            out_shape=(shape((16, 128)), shape((count, 16, 128), jnp.bfloat16)),
            in_specs=[VM] * (3 + len(ready)),
            out_specs=(VM, VM),
            compiler_params=PARAMS,
        )(exchanged(sent), meas, live, *ready)

    sent = pl.pallas_call(
        first_kernel,
        out_shape=shape((count, 16, 128), jnp.int16),
        in_specs=[SM, VM],
        out_specs=VM,
        scratch_shapes=[F_BUF] * 8 + [L_BUF, ACC_BUF],
        compiler_params=PARAMS,
    )(block_place, volume)
    def footprints(subset, start, stop, *held):
        return pl.pallas_call(
            functools.partial(footprint_kernel, subset, start, stop),
            out_shape=(shape((LOCAL, KALL, VOX), jnp.bfloat16), shape((8, 128))),
            in_specs=[SM] + [ANY] * len(held),
            out_specs=(ANY, VM),
            scratch_shapes=[
                pltpu.VMEM((MADE, KALL, VOX), jnp.bfloat16),
                L_BUF,
                pltpu.SemaphoreType.DMA((MADE,)),
            ],
            input_output_aliases={1: 0} if held else {},
            compiler_params=PARAMS,
            cost_estimate=pl.CostEstimate(
                flops=0, bytes_accessed=(stop - start) * KALL * VOX * 2, transcendentals=0
            ),
        )(block_place, *held)

    fa, token = footprints(0, 0, FIRST)
    _, rounded = residual(sent, 0, token)
    fa, _ = footprints(0, FIRST, LOCAL, fa)
    estimate, sent = pl.pallas_call(
        middle_kernel,
        out_shape=(shape(volume.shape), shape((count, 16, 128), jnp.int16)),
        in_specs=[SM, VM, VM, ANY],
        out_specs=(VM, VM),
        scratch_shapes=[
            F_RING,
            L_BUF,
            ACC_BUF,
            RES_BUF,
            pltpu.SemaphoreType.DMA((1, DEPTH)),
        ]
        + [F_BUF] * 4,
        compiler_params=PARAMS,
    )(block_place, exchanged(rounded), volume, fa)
    fb, token = footprints(1, 0, LOCAL // 2)
    last, rounded = residual(sent, 1, token)
    fb, _ = footprints(1, LOCAL // 2, LOCAL, fb)
    final = pl.pallas_call(
        last_kernel,
        out_shape=shape(volume.shape),
        in_specs=[SM, VM, VM, ANY],
        out_specs=VM,
        scratch_shapes=[F_RING, RES_BUF, pltpu.SemaphoreType.DMA((1, DEPTH))],
        compiler_params=PARAMS,
    )(block_place, exchanged(rounded), estimate, fb)
    last = unpacked_rays(last, odd).T.reshape(1, own, RAYS_TILE * NSL)
    return final, last


def solution(mesh):
    return jax.shard_map(
        shards,
        mesh=mesh,
        in_specs=(
            P(("group", "patch"), None, None),
            P(("group", "patch")),
            P(None, "patch", None),
            P(),
        ),
        out_specs=(P(("group", "patch"), None, None), P("group", "patch", None)),
        check_vma=False,
    )
```
